128 devices in a mesh: sub: 4 (over y_lo, core), lat: 32 (over y_hi, z, x).
Axes of the slice: x: 4, y: 4 (y_hi: 2, y_lo: 2; y = y_hi * 2 + y_lo), z: 4, core: 2. Of those that a mesh axis runs over, the one named last changes fastest.
Arguments:
- noise: float32 [2, 2, 4, 3, 64, 8, 128], P(None, None, None, None, 'lat', 'sub'), may hold values from -16 to 16
- colours: int32 [2, 64, 8, 128], P(None, 'lat', 'sub'), may hold values from 0 to 15
- probe_rows: int32 [4], replicated, may hold values from 0 to 15
- links: bfloat16 [2, 4, 2, 3, 3, 64, 8, 128], P(None, None, None, None, None, 'lat'), may hold values from -2.5 to 2.5
- clover_even: bfloat16 [2, 2, 6, 6, 64, 8, 128], P(None, None, None, None, 'lat'), may hold values from -0.125 to 2, as said below
- clover_odd_inverse: bfloat16 [2, 2, 6, 6, 64, 8, 128], P(None, None, None, None, 'lat'), may hold values from -0.125 to 2, as said below
Outputs:
- loops: float32 [2, 2, 4, 64, 8, 128], P(None, None, None, 'lat', 'sub')
The draws below stay inside these ranges and needn't reach their ends.
Inputs may be any that keep to these rules, and one draw needn't show every extreme that they name: `clover_even`: each 6 x 6 block is Hermitian, with a real diagonal of 1.2 to 2.0. `clover_odd_inverse`: each 6 x 6 block is Hermitian, with a real diagonal of 1.2 to 2.0.
All inputs are finite; a program needn't handle non-finite values.
Results may differ from the reference program's by a relative error of at most 0.0003.
Values sent between devices are 32-bit elements; how exact they have to be, the bound alone decides.
No kernel may reach another device: no remote copies, remote signals or barrier semaphores. Data moves between devices by JAX's collectives and lax.ppermute only.
A program may use at most 448 MiB of HBM per device.

```python
import math
import jax
import jax.numpy as jnp
import numpy as np
from jax import lax

LX = 8
LY = 32
LZ = 8
ITERS = 2
TIME = 64
VEC = 4


def assemble_blocks(diagonal, real_off, imag_off):
    unit = jnp.eye(6, dtype=jnp.float32).reshape(1, 6, 6, 1, 1, 1)
    real_sym = 0.5 * (real_off + jnp.swapaxes(real_off, 1, 2))
    imag_anti = 0.5 * (imag_off - jnp.swapaxes(imag_off, 1, 2))
    real_part = real_sym * (1.0 - unit) + diagonal[:, :, None] * unit
    imag_part = imag_anti * (1.0 - unit)
    return jnp.stack([real_part, imag_part], axis=1).astype(jnp.bfloat16)


def draw_noise(key, part):
    key = jax.random.fold_in(key, 5)
    first = jax.random.fold_in(key, 0)
    shape = (2, 2, 4, 3, TIME, LZ, LY * LX // 2)
    position = jnp.arange(TIME, dtype=jnp.float32) / max(TIME - 1, 1)
    values = jnp.clip(jax.random.normal(first, shape, jnp.float32), -5.0, 5.0)
    ramp = jnp.exp(position * 0.5 * math.log(3.0))
    return values * ramp.reshape(TIME, 1, 1)


def draw_clover_even(key, part):
    key = jax.random.fold_in(key, 7)
    keys = jax.random.split(key, 3)
    shape = (2, 6, 6, TIME, LZ, LY * LX // 2)
    diag_shape = (2, 6, TIME, LZ, LY * LX // 2)
    real_off = jnp.clip(jax.random.uniform(keys[0], shape, jnp.float32, -0.15, 0.15), -0.125, 0.125)
    imag_off = jnp.clip(jax.random.uniform(keys[1], shape, jnp.float32, -0.15, 0.15), -0.125, 0.125)
    diagonal = jax.random.uniform(keys[2], diag_shape, jnp.float32, 1.2, 2.0)
    return assemble_blocks(diagonal, real_off, imag_off)


def draw_clover_odd_inverse(key, part):
    key = jax.random.fold_in(key, 9)
    keys = jax.random.split(key, 3)
    shape = (2, 6, 6, TIME, LZ, LY * LX // 2)
    diag_shape = (2, 6, TIME, LZ, LY * LX // 2)
    real_off = jnp.clip(jax.random.uniform(keys[0], shape, jnp.float32, -0.15, 0.15), -0.125, 0.125)
    imag_off = jnp.clip(jax.random.uniform(keys[1], shape, jnp.float32, -0.15, 0.15), -0.125, 0.125)
    diagonal = jax.random.uniform(keys[2], diag_shape, jnp.float32, 1.2, 2.0)
    return assemble_blocks(diagonal, real_off, imag_off)


def place_ends(values, own_key, least, high):
    spot = [jax.random.randint(jax.random.fold_in(own_key, axis), (), 0, length) for axis, length in enumerate(values.shape)]
    main_axis = values.shape.index(max(values.shape))
    neighbour = spot[:main_axis] + [(spot[main_axis] + 1) % values.shape[main_axis]] + spot[main_axis + 1:]
    return values.at[tuple(spot)].set(least).at[tuple(neighbour)].set(high)


def block_scale(rng, extent, pieces, least, high):
    gain = 1.0
    for axis_at, shards_of in pieces:
        heights = jax.random.uniform(jax.random.fold_in(jax.random.fold_in(rng, 6), axis_at), (shards_of,), jnp.float32, least / len(pieces), high / len(pieces))
        gain = gain * jnp.repeat(jnp.exp(heights), extent[axis_at] // shards_of).reshape((-1,) + (1,) * (len(extent) - 1 - axis_at))
    return gain


def centred(key, shape, width, bound, pieces=(), kind=jnp.bfloat16):
    drawn = jax.random.normal(key, shape, jnp.float32) * width
    if len(pieces) > 0:
        drawn = block_scale(key, shape, pieces, -0.22, 0.18) * drawn
    return jnp.clip(drawn, min=-bound, max=bound).astype(kind)


def setup_inputs(seed: int = 0) -> dict:
    splits = jax.random.split(jax.random.key(seed), 7)
    noise = draw_noise(jax.random.fold_in(splits[6], 71), 0)
    colours = place_ends(jax.random.randint(splits[1], (2, TIME, LZ, LY * LX // 2), 0, 16), jax.random.fold_in(splits[1], 1), 0, 15).astype(jnp.int32)
    probe_rows = place_ends(jax.random.randint(splits[2], (VEC,), 0, 16), jax.random.fold_in(splits[2], 1), 0, 15).astype(jnp.int32)
    links = centred(splits[3], (2, 4, 2, 3, 3, TIME, LZ, LY * LX // 2), 6 ** -0.5, 2.5, ((5, 32),))
    clover_even = draw_clover_even(jax.random.fold_in(splits[6], 71), 0)
    clover_odd_inverse = draw_clover_odd_inverse(jax.random.fold_in(splits[6], 71), 0)
    return dict(noise=noise, colours=colours, probe_rows=probe_rows, links=links, clover_even=clover_even, clover_odd_inverse=clover_odd_inverse)


KAPPA = 0.135


def spin_block(upper_right, lower_left):
    return np.array([[0, 0, upper_right[0][0], upper_right[0][1]], [0, 0, upper_right[1][0], upper_right[1][1]], [lower_left[0][0], lower_left[0][1], 0, 0], [lower_left[1][0], lower_left[1][1], 0, 0]], dtype=complex)


def gamma_tables():
    pauli_set = [np.array([[0, 1], [1, 0]], dtype=complex), np.array([[0, -1j], [1j, 0]], dtype=complex), np.array([[1, 0], [0, -1]], dtype=complex)]
    unit_two = np.eye(2, dtype=complex)
    matrices = [spin_block(-1j * sigma, 1j * sigma) for sigma in pauli_set]
    matrices.append(spin_block(unit_two, unit_two))
    stacked = np.stack(matrices)
    return jnp.asarray(stacked.real.astype(np.float32)), jnp.asarray(stacked.imag.astype(np.float32))


def spin_apply(table_real, table_imag, vector):
    vec_real, vec_imag = vector[:, 0], vector[:, 1]
    highest = lax.Precision.HIGHEST
    real_part = jnp.einsum('st,vt...->vs...', table_real, vec_real, precision=highest) - jnp.einsum('st,vt...->vs...', table_imag, vec_imag, precision=highest)
    imag_part = jnp.einsum('st,vt...->vs...', table_real, vec_imag, precision=highest) + jnp.einsum('st,vt...->vs...', table_imag, vec_real, precision=highest)
    return jnp.stack([real_part, imag_part], axis=1)


def colour_apply(link, vector, adjoint=False):
    link_real, link_imag = link[0], link[1]
    if adjoint:
        link_real = jnp.swapaxes(link_real, 0, 1)
        link_imag = -jnp.swapaxes(link_imag, 0, 1)
    vec_real = vector[:, 0][:, :, None]
    vec_imag = vector[:, 1][:, :, None]
    link_real = link_real[None, None]
    link_imag = link_imag[None, None]
    real_part = jnp.sum(link_real * vec_real - link_imag * vec_imag, axis=3)
    imag_part = jnp.sum(link_real * vec_imag + link_imag * vec_real, axis=3)
    return jnp.stack([real_part, imag_part], axis=1)


def clover_apply(block, vector):
    shape = vector.shape
    halves = vector.reshape(shape[:2] + (2, 6) + shape[4:])
    half_real = halves[:, 0][:, :, None]
    half_imag = halves[:, 1][:, :, None]
    block_real = block[:, 0][None]
    block_imag = block[:, 1][None]
    real_part = jnp.sum(block_real * half_real - block_imag * half_imag, axis=3)
    imag_part = jnp.sum(block_real * half_imag + block_imag * half_real, axis=3)
    return jnp.stack([real_part, imag_part], axis=1).reshape(shape)


def chirality(vector):
    signs = jnp.array([1.0, 1.0, -1.0, -1.0], dtype=jnp.float32).reshape((1, 1, 4) + (1,) * (vector.ndim - 3))
    return vector * signs


def parity_rows(time_local, depth_local, time_start, depth_start, parity):
    times = jnp.arange(time_local, dtype=jnp.int32)[:, None, None] + time_start
    depths = jnp.arange(depth_local, dtype=jnp.int32)[None, :, None] + depth_start
    plane = (jnp.arange(LY * (LX // 2), dtype=jnp.int32) // (LX // 2))[None, None, :]
    return (times + depths + plane + parity) % 2


def roll_plane(field, hop_dir, offset, rows):
    if hop_dir == 0:
        shaped = field.reshape(field.shape[:-1] + (LY, LX // 2))
        rolled = jnp.roll(shaped, -offset, axis=-1).reshape(field.shape)
        wanted = 1 if offset > 0 else 0
        return jnp.where(rows == wanted, rolled, field)
    return jnp.roll(field, -offset * (LX // 2), axis=-1)


def hop(source, link_dst, link_src, rows, fetch):
    table_real, table_imag = gamma_tables()
    total = jnp.zeros_like(source)
    for hop_dir in range(4):
        forward = colour_apply(link_dst[hop_dir], fetch(source, hop_dir, 1, rows))
        backward = fetch(colour_apply(link_src[hop_dir], source, True), hop_dir, -1, rows)
        total = total + (forward + backward) - spin_apply(table_real[hop_dir], table_imag[hop_dir], forward - backward)
    return total


def schur(vector, links, clover_even, clover_odd_inverse, rows, fetch):
    odd_field = hop(vector, links[1], links[0], rows[1], fetch)
    odd_field = clover_apply(clover_odd_inverse, odd_field)
    returned = hop(odd_field, links[0], links[1], rows[0], fetch)
    return clover_apply(clover_even, vector) - KAPPA * KAPPA * returned


def inner(left, right):
    return jnp.sum(left * right, axis=tuple(range(1, left.ndim)))


def scale(coef, field):
    return coef.reshape((-1,) + (1,) * (field.ndim - 1)) * field


def make_probes(noise, colours, probe_rows):
    masked = jnp.bitwise_and(probe_rows.reshape(1, -1, 1, 1, 1), colours[:, None])
    bit_count = jnp.zeros_like(masked)
    for bit_index in range(4):
        bit_count = bit_count + jnp.bitwise_and(jnp.right_shift(masked, bit_index), 1)
    signs = (1 - 2 * (bit_count % 2)).astype(jnp.float32)
    return noise[:, None] * signs[:, :, None, None, None]


def trace_loops(probes, solved):
    table_real, table_imag = gamma_tables()
    per_parity = []
    for parity in range(2):
        left = probes[parity]
        right = solved[parity]
        columns = []
        for hop_dir in range(4):
            turned = spin_apply(table_real[hop_dir], table_imag[hop_dir], right)
            real_part = jnp.sum(left[:, 0] * turned[:, 0] + left[:, 1] * turned[:, 1], axis=(0, 1, 2))
            imag_part = jnp.sum(left[:, 0] * turned[:, 1] - left[:, 1] * turned[:, 0], axis=(0, 1, 2))
            columns.append(jnp.stack([real_part, imag_part]))
        per_parity.append(jnp.stack(columns, axis=1))
    return jnp.stack(per_parity)


def fetch_whole(field, hop_dir, offset, rows):
    if hop_dir < 2:
        return roll_plane(field, hop_dir, offset, rows)
    if hop_dir == 2:
        return jnp.roll(field, -offset, axis=-2)
    length = field.shape[-3]
    edge = length - 1 if offset > 0 else 0
    rolled = jnp.roll(field, -offset, axis=-3)
    signs = jnp.where(jnp.arange(length, dtype=jnp.int32) == edge, -1.0, 1.0).astype(jnp.float32).reshape(length, 1, 1)
    return rolled * signs


def solve_whole(fields, links, clover_even, clover_odd_inverse, rows):
    def apply_m(vector):
        return schur(vector, links, clover_even, clover_odd_inverse, rows, fetch_whole)

    def apply_mdag(vector):
        return chirality(apply_m(chirality(vector)))

    probe_even, probe_odd = fields[0], fields[1]
    rhs = probe_even + KAPPA * hop(clover_apply(clover_odd_inverse, probe_odd), links[0], links[1], rows[0], fetch_whole)
    residual = apply_mdag(rhs)
    solution = jnp.zeros_like(residual)
    search = residual
    norm_now = inner(residual, residual)
    for iteration in range(ITERS):
        image = apply_mdag(apply_m(search))
        alpha = norm_now / inner(search, image)
        solution = solution + scale(alpha, search)
        residual = residual - scale(alpha, image)
        if iteration + 1 < ITERS:
            norm_next = inner(residual, residual)
            search = residual + scale(norm_next / norm_now, search)
            norm_now = norm_next
    odd_part = clover_apply(clover_odd_inverse, probe_odd + KAPPA * hop(solution, links[1], links[0], rows[1], fetch_whole))
    return jnp.stack([solution, odd_part])


def reference(noise, colours, probe_rows, links, clover_even, clover_odd_inverse):
    probes = make_probes(noise, colours, probe_rows)
    rows = (parity_rows(noise.shape[4], noise.shape[5], 0, 0, 0), parity_rows(noise.shape[4], noise.shape[5], 0, 0, 1))

    def solve_one(fields):
        return solve_whole(fields, links, clover_even, clover_odd_inverse, rows)

    stacked = lax.map(solve_one, jnp.moveaxis(probes, 1, 0)[:, :, None])
    solved = jnp.moveaxis(stacked[:, :, 0], 0, 1)
    return trace_loops(probes, solved)
```

```python
import functools

import jax
import jax.numpy as jnp
from jax import lax
from jax.experimental import pallas as pl
from jax.experimental.pallas import tpu as pltpu
from jax.sharding import PartitionSpec as P

KAPPA = 0.135
F32 = jnp.float32

TURN = (
    ((1, 1), (0, 1)),
    ((1, 0), (0, 2)),
    ((0, 1), (1, 3)),
    ((0, 0), (1, 0)),
)
PAIRS = tuple((i, j) for i in range(6) for j in range(i + 1, 6))


def plus(x, y, power):
    power = power % 4
    if power == 0:
        return (x[0] + y[0], x[1] + y[1])
    if power == 1:
        return (x[0] - y[1], x[1] + y[0])
    if power == 2:
        return (x[0] - y[0], x[1] - y[1])
    return (x[0] + y[1], x[1] - y[0])


def mul(x, y):
    return (x[0] * y[0] - x[1] * y[1], x[0] * y[1] + x[1] * y[0])


def mul_conj(x, y):
    return (x[0] * y[0] + x[1] * y[1], x[0] * y[1] - x[1] * y[0])


def project(spinor, hop_dir, sign):
    if hop_dir == 3:
        extra = 0 if sign > 0 else 2
    else:
        extra = 2 if sign > 0 else 0
    return [
        [
            plus(spinor[s][a], spinor[2 + TURN[hop_dir][s][0]][a], TURN[hop_dir][s][1] + extra)
            for a in range(3)
        ]
        for s in range(2)
    ]


def expand_onto(total, half, hop_dir, sign):
    extra = 0 if sign > 0 else 2
    for s in range(2):
        source, power = TURN[hop_dir][s]
        for a in range(3):
            total[s][a] = half[s][a] if total[s][a] is None else plus(total[s][a], half[s][a], 0)
            if total[2 + s][a] is None:
                zero = jnp.zeros_like(half[source][a][0])
                total[2 + s][a] = plus((zero, zero), half[source][a], power + extra)
            else:
                total[2 + s][a] = plus(total[2 + s][a], half[source][a], power + extra)
    return total


def link_at(links, parity, hop_dir, time):
    return [
        [
            (
                links[parity, hop_dir, 0, i, j, time].astype(F32),
                links[parity, hop_dir, 1, i, j, time].astype(F32),
            )
            for j in range(3)
        ]
        for i in range(3)
    ]


def link_mul(link, half):
    out = []
    for s in range(2):
        row = []
        for i in range(3):
            total = mul(link[i][0], half[s][0])
            for j in (1, 2):
                total = plus(total, mul(link[i][j], half[s][j]), 0)
            row.append(total)
        out.append(row)
    return out


def link_mul_adj(link, half):
    out = []
    for s in range(2):
        row = []
        for i in range(3):
            total = mul_conj(link[0][i], half[s][0])
            for j in (1, 2):
                total = plus(total, mul_conj(link[j][i], half[s][j]), 0)
            row.append(total)
        out.append(row)
    return out


def shift_x(half, time, parity, offset):
    shape = (8, 128)
    depth = lax.broadcasted_iota(jnp.int32, shape, 0)
    lane = lax.broadcasted_iota(jnp.int32, shape, 1)
    row = (depth + lane // 4 + (time + parity)) % 2
    wanted = 1 if offset > 0 else 0
    moved = (lane // 4) * 4 + (lane + offset) % 4
    index = jnp.where(row == wanted, moved, lane)
    pick = lambda v: jnp.take_along_axis(v, index, axis=1, mode="promise_in_bounds")
    return [[(pick(v[0]), pick(v[1])) for v in r] for r in half]


def shift(half, hop_dir, time, parity, offset):
    if hop_dir == 0:
        return shift_x(half, time, parity, offset)
    if hop_dir == 1:
        pick = lambda v: pltpu.roll(v, (-4 * offset) % 128, 1)
    else:
        pick = lambda v: pltpu.roll(v, (-offset) % 8, 0)
    return [[(pick(v[0]), pick(v[1])) for v in r] for r in half]


def load_spinor(ref, *lead):
    return [
        [(ref[(*lead, s * 3 + a)], ref[(*lead, 12 + s * 3 + a)]) for a in range(3)]
        for s in range(4)
    ]


def store_spinor(ref, spinor, *lead):
    for s in range(4):
        for a in range(3):
            ref[(*lead, s * 3 + a)] = spinor[s][a][0]
            ref[(*lead, 12 + s * 3 + a)] = spinor[s][a][1]


def load_half(ref, base=0):
    return [
        [(ref[base + s * 3 + a], ref[base + 6 + s * 3 + a]) for a in range(3)] for s in range(2)
    ]


def store_half(ref, half, base, factor):
    for s in range(2):
        for a in range(3):
            ref[base + s * 3 + a] = half[s][a][0] * factor
            ref[base + 6 + s * 3 + a] = half[s][a][1] * factor


def scaled_half(half, factor):
    return [[(v[0] * factor, v[1] * factor) for v in r] for r in half]


def add_half(x, y):
    return [[plus(x[s][a], y[s][a], 0) for a in range(3)] for s in range(2)]


def hop_at(field, links, time, parity, dagger, high=None, low=None):
    forward, backward = (1, -1) if dagger else (-1, 1)
    total = [[None] * 3 for _ in range(4)]
    own = load_spinor(field, time)
    for hop_dir in range(3):
        half = shift(project(own, hop_dir, forward), hop_dir, time, parity, 1)
        half = link_mul(link_at(links, parity, hop_dir, time), half)
        expand_onto(total, half, hop_dir, forward)
        half = link_mul_adj(
            link_at(links, 1 - parity, hop_dir, time), project(own, hop_dir, backward)
        )
        expand_onto(total, shift(half, hop_dir, time, parity, -1), hop_dir, backward)
    if time == 0:
        half = project(load_spinor(field, 1), 3, forward)
        expand_onto(total, link_mul(link_at(links, parity, 3, 0), half), 3, forward)
        if low is not None:
            expand_onto(total, low, 3, backward)
    else:
        half = project(load_spinor(field, 0), 3, backward)
        expand_onto(total, link_mul_adj(link_at(links, 1 - parity, 3, 0), half), 3, backward)
        if high is not None:
            expand_onto(total, link_mul(link_at(links, parity, 3, 1), high), 3, forward)
    return total


def block_at(clover, chiral, time):
    diagonal = [clover[chiral, 0, i, i, time].astype(F32) for i in range(6)]
    upper = {
        (i, j): (
            clover[chiral, 0, i, j, time].astype(F32),
            clover[chiral, 1, i, j, time].astype(F32),
        )
        for i, j in PAIRS
    }
    return diagonal, upper


def block_packed(ref):
    diagonal = [ref[i] for i in range(6)]
    upper = {pair: (ref[6 + 2 * n], ref[7 + 2 * n]) for n, pair in enumerate(PAIRS)}
    return diagonal, upper


def block_mul(block, half):
    diagonal, upper = block
    flat = half[0] + half[1]
    out = [(diagonal[i] * flat[i][0], diagonal[i] * flat[i][1]) for i in range(6)]
    for i, j in PAIRS:
        out[i] = plus(out[i], mul(upper[i, j], flat[j]), 0)
        out[j] = plus(out[j], mul_conj(upper[i, j], flat[i]), 0)
    return [out[:3], out[3:]]


def clover_at(clover, spinor, time):
    return block_mul(block_at(clover, 0, time), spinor[:2]) + block_mul(
        block_at(clover, 1, time), spinor[2:]
    )


def edge_signs():
    position = lax.axis_index("lat")
    last = lax.axis_size("lat") - 1
    at_first = jnp.where(position == 0, -1.0, 1.0).astype(F32)
    at_last = jnp.where(position == last, -1.0, 1.0).astype(F32)
    return at_first, at_last


def begin_schur(vector, links, odd_inverse, dagger, partial, high, low):
    forward, backward = (1, -1) if dagger else (-1, 1)
    at_first, at_last = edge_signs()
    for time in range(2):
        store_spinor(
            partial, clover_at(odd_inverse, hop_at(vector, links, time, 1, dagger), time), time
        )
    store_half(high, project(load_spinor(vector, 0), 3, forward), 0, at_first)
    store_half(high, project(load_spinor(partial, 0), 3, forward), 12, at_first)
    half = link_mul_adj(link_at(links, 0, 3, 1), project(load_spinor(vector, 1), 3, backward))
    store_half(low, half, 0, at_last)
    half = link_mul_adj(link_at(links, 1, 3, 1), project(load_spinor(partial, 1), 3, backward))
    store_half(low, half, 12, at_last)


def end_schur(
    vector, partial, sent_high, sent_low, got_high, got_low, around_high, around_low,
    links, even, odd_inverse, dagger, odd_field, result,
):
    forward, backward = (1, -1) if dagger else (-1, 1)
    at_first, at_last = edge_signs()
    for time in range(2):
        if time == 0:
            half, sign = load_half(got_low), backward
        else:
            half = link_mul(link_at(links, 1, 3, 1), load_half(got_high))
            sign = forward
        own = load_spinor(partial, time)
        top = block_mul(block_at(odd_inverse, 0, time), half)
        bottom = block_mul(block_at(odd_inverse, 1, time), half)
        whole = [[plus(own[s][a], top[s][a], 0) for a in range(3)] for s in range(2)] + [
            [plus(own[2 + s][a], bottom[s][a], 0 if sign > 0 else 2) for a in range(3)]
            for s in range(2)
        ]
        store_spinor(odd_field, whole, time)
    back = block_mul(block_packed(around_high), load_half(sent_low))
    high = add_half(load_half(got_high, 12), scaled_half(back, at_last))
    back = block_mul(block_packed(around_low), load_half(sent_high))
    low = add_half(load_half(got_low, 12), scaled_half(back, at_first))
    for time in range(2):
        returned = hop_at(odd_field, links, time, 0, dagger, high, low)
        direct = clover_at(even, load_spinor(vector, time), time)
        factor = KAPPA * KAPPA
        store_spinor(
            result,
            [
                [
                    (
                        direct[s][a][0] - factor * returned[s][a][0],
                        direct[s][a][1] - factor * returned[s][a][1],
                    )
                    for a in range(3)
                ]
                for s in range(4)
            ],
            time,
        )


def around_kernel(links, odd_inverse, high, low):
    blocks = []
    for time in range(2):
        diagonal0, upper0 = block_at(odd_inverse, 0, time)
        diagonal1, upper1 = block_at(odd_inverse, 1, time)
        blocks.append(
            (
                [x - y for x, y in zip(diagonal0, diagonal1)],
                {pair: plus(upper0[pair], upper1[pair], 2) for pair in PAIRS},
            )
        )
    diagonal, upper = blocks[0]
    for i in range(6):
        high[i] = diagonal[i]
    for n, pair in enumerate(PAIRS):
        high[6 + 2 * n], high[7 + 2 * n] = upper[pair]
    diagonal, upper = blocks[1]

    def entry(i, j):
        if i == j:
            return (diagonal[i], jnp.zeros_like(diagonal[i]))
        if i < j:
            return upper[i, j]
        value = upper[j, i]
        return (value[0], -value[1])

    link = link_at(links, 1, 3, 1)
    for s0, s1 in ((0, 0), (0, 1), (1, 1)):
        right = [[None] * 3 for _ in range(3)]
        for a in range(3):
            for b in range(3):
                total = mul(entry(s0 * 3 + a, s1 * 3), link[0][b])
                for c in (1, 2):
                    total = plus(total, mul(entry(s0 * 3 + a, s1 * 3 + c), link[c][b]), 0)
                right[a][b] = total
        for a in range(3):
            for b in range(3):
                if s0 == s1 and a > b:
                    continue
                total = mul_conj(link[0][a], right[0][b])
                for c in (1, 2):
                    total = plus(total, mul_conj(link[c][a], right[c][b]), 0)
                i, j = s0 * 3 + a, s1 * 3 + b
                if i == j:
                    low[i] = total[0]
                else:
                    n = PAIRS.index((i, j))
                    low[6 + 2 * n], low[7 + 2 * n] = total


def vector_index():
    upper = lax.axis_index("lat") // (lax.axis_size("lat") // 2)
    return jnp.bitwise_xor(lax.axis_index("sub"), 2 * upper)


def start_kernel(probe_rows, gathered, links, odd_inverse, probes, turned, rhs, high, low, raw):
    for q in range(4):
        raw[:, :, 2 * q : 2 * q + 2, :] = gathered[q]
    probe_row = probe_rows[vector_index()]
    at_first, at_last = edge_signs()
    for parity in range(2):
        for time in range(2):
            masked = jnp.bitwise_and(raw[48 + parity, time].astype(jnp.int32), probe_row)
            masked = jnp.bitwise_xor(masked, jnp.right_shift(masked, 2))
            masked = jnp.bitwise_xor(masked, jnp.right_shift(masked, 1))
            sign = (1 - 2 * jnp.bitwise_and(masked, 1)).astype(F32)
            for n in range(24):
                probes[parity, time, n] = raw[parity * 24 + n, time] * sign
    for time in range(2):
        store_spinor(turned, clover_at(odd_inverse, load_spinor(probes, 1, time), time), time)
    for time in range(2):
        total = hop_at(turned, links, time, 0, False)
        own = load_spinor(probes, 0, time)
        store_spinor(
            rhs,
            [
                [
                    (own[s][a][0] + KAPPA * total[s][a][0], own[s][a][1] + KAPPA * total[s][a][1])
                    for a in range(3)
                ]
                for s in range(4)
            ],
            time,
        )
    store_half(high, project(load_spinor(turned, 0), 3, -1), 0, at_first)
    half = link_mul_adj(link_at(links, 1, 3, 1), project(load_spinor(turned, 1), 3, 1))
    store_half(low, half, 0, at_last)


def rhs_kernel(partial, got_high, got_low, links, odd_inverse, rhs, odd, high, low):
    half = scaled_half(load_half(got_low), KAPPA)
    store_spinor(rhs, expand_onto(load_spinor(partial, 0), half, 3, 1), 0)
    half = scaled_half(link_mul(link_at(links, 0, 3, 1), load_half(got_high)), KAPPA)
    store_spinor(rhs, expand_onto(load_spinor(partial, 1), half, 3, -1), 1)
    begin_schur(rhs, links, odd_inverse, True, odd, high, low)


def step_kernel(
    dagger,
    vector, partial, sent_high, sent_low, got_high, got_low, around_high, around_low,
    links, even, odd_inverse,
    result, odd_field, odd, high, low,
):
    end_schur(
        vector, partial, sent_high, sent_low, got_high, got_low, around_high, around_low,
        links, even, odd_inverse, dagger, odd_field, result,
    )
    begin_schur(result, links, odd_inverse, not dagger, odd, high, low)


def column_sum(left, right):
    total = None
    for time in range(2):
        for n in range(24):
            term = left(time, n) * right(time, n)
            total = term if total is None else total + term
    return jnp.sum(total, axis=0, keepdims=True)


def last_kernel(
    vector, partial, sent_high, sent_low, got_high, got_low, around_high, around_low,
    links, even, odd_inverse, first, image,
    odd_field, sums, result,
):
    end_schur(
        vector, partial, sent_high, sent_low, got_high, got_low, around_high, around_low,
        links, even, odd_inverse, False, odd_field, result,
    )
    first_at = lambda time, n: first[time, n]
    image_at = lambda time, n: image[time, n]
    vector_at = lambda time, n: vector[time, n]
    norm = column_sum(first_at, first_at)
    image_norm = column_sum(image_at, image_at)
    norm_all = jnp.sum(norm, axis=1, keepdims=True)
    about = jnp.sum(image_norm, axis=1, keepdims=True) / jnp.where(norm_all > 0, norm_all, 1.0)
    about = jnp.broadcast_to(about, (1, 128))
    about_full = jnp.broadcast_to(about, (8, 128))
    rest_at = lambda time, n: vector[time, n] - about_full * first[time, n]
    image_rest_at = lambda time, n: result[time, n] - about_full * image[time, n]
    rows = [
        norm,
        column_sum(first_at, vector_at),
        about,
        column_sum(rest_at, rest_at),
        column_sum(rest_at, first_at),
        column_sum(image_rest_at, image_rest_at),
        column_sum(image_rest_at, image_at),
        image_norm,
    ]
    block = jnp.concatenate(rows, axis=0)
    for n in range(sums.shape[0]):
        sums[n] = block


def trace_kernel(sums, probes, turned, first, first_odd, second, second_odd, out):
    whole = lambda x: jnp.sum(jnp.sum(x, axis=0, keepdims=True), axis=1, keepdims=True)
    row = [sums[:, n, :] for n in range(8)]
    norm, crossed, about, rest, rest_first, image_rest, image_cross, image_norm = row
    norm_all = whole(norm)
    inverse = whole(crossed) / norm_all
    alpha = norm_all / whole(crossed)
    off = about - inverse
    norm_next = alpha * alpha * whole(rest + 2.0 * off * rest_first + off * off * norm)
    beta = norm_next / norm_all
    off = about - (1.0 + beta) / alpha
    curved = alpha * alpha * whole(
        image_rest + 2.0 * off * image_cross + off * off * image_norm
    )
    alpha_next = norm_next / curved
    alpha = jnp.broadcast_to(alpha, (8, 128))
    alpha_next = jnp.broadcast_to(alpha_next, (8, 128))
    beta = jnp.broadcast_to(beta, (8, 128))
    for time in range(2):
        for parity in range(2):
            values = []
            for n in range(24):
                if parity == 0:
                    base, other = first[time, n], second[time, n]
                else:
                    base, other = first_odd[time, n], second_odd[time, n]
                search = (base - alpha * other) + beta * base
                value = alpha * base + alpha_next * search
                if parity == 1:
                    value = turned[time, n] + KAPPA * value
                values.append(value)
            right = [
                [(values[s * 3 + a], values[12 + s * 3 + a]) for a in range(3)] for s in range(4)
            ]
            left = load_spinor(probes, parity, time)

            def dot(s, r):
                total = mul_conj(left[s][0], right[r][0])
                for a in (1, 2):
                    total = plus(total, mul_conj(left[s][a], right[r][a]), 0)
                return total

            up = [[dot(s, 2 + r) for r in range(2)] for s in range(2)]
            down = [[dot(2 + s, r) for r in range(2)] for s in range(2)]
            x_sum = plus(plus(down[0][1], down[1][0], 0), plus(up[0][1], up[1][0], 0), 2)
            y_sum = plus(plus(down[0][1], down[1][0], 2), plus(up[0][1], up[1][0], 2), 2)
            z_sum = plus(plus(down[0][0], down[1][1], 2), plus(up[0][0], up[1][1], 2), 2)
            t_sum = plus(plus(down[0][0], down[1][1], 0), plus(up[0][0], up[1][1], 0), 0)
            columns = ((-x_sum[1], x_sum[0]), y_sum, (-z_sum[1], z_sum[0]), t_sum)
            for hop_dir in range(4):
                for part in range(2):
                    value = columns[hop_dir][part]
                    for q in range(4):
                        out[q, parity * 8 + part * 4 + hop_dir, time] = value[2 * q : 2 * q + 2]


VMEM = pl.BlockSpec(memory_space=pltpu.VMEM)
SMEM = pl.BlockSpec(memory_space=pltpu.SMEM)


def call(kernel, name, shapes, scalars, arrays, scratch=()):
    return pl.pallas_call(
        kernel,
        out_shape=tuple(jax.ShapeDtypeStruct(s, F32) for s in shapes),
        in_specs=[SMEM] * len(scalars) + [VMEM] * len(arrays),
        out_specs=tuple(VMEM for _ in shapes),
        scratch_shapes=[pltpu.VMEM(s, F32) for s in scratch],
        compiler_params=pltpu.CompilerParams(vmem_limit_bytes=24 * 1024 * 1024),
        name=name,
    )(*scalars, *arrays)


FIELD = (2, 24, 8, 128)
EDGE = (24, 8, 128)


def to_neighbour(array, by):
    length, subs = lax.axis_size("lat"), lax.axis_size("sub")
    flip = lambda place: 2 * (place // (length // 2))
    pairs = []
    for place in range(length):
        target = (place + by) % length
        for vector in range(subs):
            pairs.append(
                (
                    (vector ^ flip(place)) * length + place,
                    (vector ^ flip(target)) * length + target,
                )
            )
    return lax.ppermute(array, ("sub", "lat"), pairs)


def exchange(high, low):
    return to_neighbour(high, -1), to_neighbour(low, 1)


def shards(noise, colours, probe_rows, links, clover_even, clover_odd_inverse):
    own = jnp.concatenate(
        [noise.reshape((48,) + noise.shape[4:]), colours.astype(F32)], axis=0
    )
    gathered = lax.all_gather(own, "sub")
    around = call(
        around_kernel, "around", ((36, 8, 128),) * 2, (), (links, clover_odd_inverse)
    )
    around = exchange(*around)
    probes, turned, partial, high, low = call(
        start_kernel,
        "start",
        ((2,) + FIELD, FIELD, FIELD, (12, 8, 128), (12, 8, 128)),
        (probe_rows,),
        (gathered, links, clover_odd_inverse),
        ((50, 2, 8, 128),),
    )
    got = exchange(high, low)
    vector, odd, high, low = call(
        rhs_kernel, "rhs", (FIELD, FIELD, EDGE, EDGE), (), (partial, *got, links, clover_odd_inverse)
    )
    kept = []
    for step in range(3):
        got = exchange(high, low)
        result, odd_field, odd, high, low = call(
            functools.partial(step_kernel, step % 2 == 0),
            "step%d" % step,
            (FIELD, FIELD, FIELD, EDGE, EDGE),
            (),
            (vector, odd, high, low, *got, *around, links, clover_even, clover_odd_inverse),
        )
        kept.append((result, odd_field))
        vector = result
    first, image, second = kept[0][0], kept[1][0], kept[2][0]
    first_odd = kept[1][1]
    got = exchange(high, low)
    second_odd, sums = call(
        last_kernel,
        "last",
        (FIELD, (lax.axis_size("lat"), 8, 128)),
        (),
        (
            second, odd, high, low, *got, *around, links, clover_even, clover_odd_inverse,
            first, image,
        ),
        (FIELD,),
    )
    return probes, turned, first, first_odd, second, second_odd, sums


def gather_sums(sums):
    length, subs = lax.axis_size("lat"), lax.axis_size("sub")
    groups = [
        [(vector ^ (2 * (place // (length // 2)))) * length + place for place in range(length)]
        for vector in range(subs)
    ]
    return lax.all_to_all(
        sums, ("sub", "lat"), 0, 0, tiled=True, axis_index_groups=groups
    )


def whole(noise, colours, probe_rows, links, clover_even, clover_odd_inverse):
    probes, turned, first, first_odd, second, second_odd, sums = shards(
        noise, colours, probe_rows, links, clover_even, clover_odd_inverse
    )
    sums = gather_sums(sums)
    (traces,) = call(
        trace_kernel,
        "trace",
        ((4, 16, 2, 2, 128),),
        (),
        (sums, probes, turned, first, first_odd, second, second_odd),
    )
    traces = lax.all_to_all(traces, "sub", 0, 0, tiled=True)
    return jnp.sum(traces, axis=0).reshape(2, 2, 4, 2, 2, 128)


def solution(mesh):
    placed = (
        P(None, None, None, None, "lat", "sub", None),
        P(None, "lat", "sub", None),
        P(),
        P(None, None, None, None, None, "lat", None, None),
        P(None, None, None, None, "lat", None, None),
        P(None, None, None, None, "lat", None, None),
    )
    return jax.shard_map(
        whole,
        mesh=mesh,
        in_specs=placed,
        out_specs=P(None, None, None, "lat", "sub", None),
        check_vma=False,
    )
```

```python
import functools

import jax
import jax.numpy as jnp
from jax import lax
from jax.experimental import pallas as pl
from jax.experimental.pallas import tpu as pltpu
from jax.sharding import PartitionSpec as P

KAPPA = 0.135
F32 = jnp.float32

TURN = (
    ((1, 1), (0, 1)),
    ((1, 0), (0, 2)),
    ((0, 1), (1, 3)),
    ((0, 0), (1, 0)),
)
PAIRS = tuple((i, j) for i in range(6) for j in range(i + 1, 6))


def plus(x, y, power):
    power = power % 4
    if power == 0:
        return (x[0] + y[0], x[1] + y[1])
    if power == 1:
        return (x[0] - y[1], x[1] + y[0])
    if power == 2:
        return (x[0] - y[0], x[1] - y[1])
    return (x[0] + y[1], x[1] - y[0])


def mul(x, y):
    return (x[0] * y[0] - x[1] * y[1], x[0] * y[1] + x[1] * y[0])


def mul_conj(x, y):
    return (x[0] * y[0] + x[1] * y[1], x[0] * y[1] - x[1] * y[0])


def project(spinor, hop_dir, sign):
    if hop_dir == 3:
        extra = 0 if sign > 0 else 2
    else:
        extra = 2 if sign > 0 else 0
    return [
        [
            plus(spinor[s][a], spinor[2 + TURN[hop_dir][s][0]][a], TURN[hop_dir][s][1] + extra)
            for a in range(3)
        ]
        for s in range(2)
    ]


def expand_onto(total, half, hop_dir, sign):
    extra = 0 if sign > 0 else 2
    for s in range(2):
        source, power = TURN[hop_dir][s]
        for a in range(3):
            total[s][a] = half[s][a] if total[s][a] is None else plus(total[s][a], half[s][a], 0)
            if total[2 + s][a] is None:
                zero = jnp.zeros_like(half[source][a][0])
                total[2 + s][a] = plus((zero, zero), half[source][a], power + extra)
            else:
                total[2 + s][a] = plus(total[2 + s][a], half[source][a], power + extra)
    return total


def link_at(links, parity, hop_dir, time):
    return [
        [
            (
                links[parity, hop_dir, 0, i, j, time].astype(F32),
                links[parity, hop_dir, 1, i, j, time].astype(F32),
            )
            for j in range(3)
        ]
        for i in range(3)
    ]


def link_mul(link, half):
    out = []
    for s in range(2):
        row = []
        for i in range(3):
            total = mul(link[i][0], half[s][0])
            for j in (1, 2):
                total = plus(total, mul(link[i][j], half[s][j]), 0)
            row.append(total)
        out.append(row)
    return out


def link_mul_adj(link, half):
    out = []
    for s in range(2):
        row = []
        for i in range(3):
            total = mul_conj(link[0][i], half[s][0])
            for j in (1, 2):
                total = plus(total, mul_conj(link[j][i], half[s][j]), 0)
            row.append(total)
        out.append(row)
    return out


def shift_x(half, time, parity, offset):
    shape = (8, 128)
    depth = lax.broadcasted_iota(jnp.int32, shape, 0)
    lane = lax.broadcasted_iota(jnp.int32, shape, 1)
    row = (depth + lane // 4 + (time + parity)) % 2
    wanted = 1 if offset > 0 else 0
    moved = (lane // 4) * 4 + (lane + offset) % 4
    index = jnp.where(row == wanted, moved, lane)
    pick = lambda v: jnp.take_along_axis(v, index, axis=1, mode="promise_in_bounds")
    return [[(pick(v[0]), pick(v[1])) for v in r] for r in half]


def shift(half, hop_dir, time, parity, offset):
    if hop_dir == 0:
        return shift_x(half, time, parity, offset)
    if hop_dir == 1:
        pick = lambda v: pltpu.roll(v, (-4 * offset) % 128, 1)
    else:
        pick = lambda v: pltpu.roll(v, (-offset) % 8, 0)
    return [[(pick(v[0]), pick(v[1])) for v in r] for r in half]


def load_spinor(ref, *lead):
    return [
        [(ref[(*lead, s * 3 + a)], ref[(*lead, 12 + s * 3 + a)]) for a in range(3)]
        for s in range(4)
    ]


def store_spinor(ref, spinor, *lead):
    for s in range(4):
        for a in range(3):
            ref[(*lead, s * 3 + a)] = spinor[s][a][0]
            ref[(*lead, 12 + s * 3 + a)] = spinor[s][a][1]


class Swapped:

    def __init__(self, far, near):
        self.far, self.near = far, near
        self.odd = lax.rem(lax.axis_index("lat"), 2) == 1

    def high(self, n):
        return lax.select(self.odd, self.far[n], self.near[n])

    def low(self, n):
        return lax.select(self.odd, self.near[n], self.far[n])

    def put(self, n, for_earlier, for_later):
        self.far[n] = lax.select(self.odd, for_later, for_earlier)
        self.near[n] = lax.select(self.odd, for_earlier, for_later)


def load_half(row, base=0):
    return [
        [(row(base + s * 3 + a), row(base + 6 + s * 3 + a)) for a in range(3)] for s in range(2)
    ]


def store_halves(edges, for_earlier, for_later, base):
    at_first, at_last = edge_signs()
    for s in range(2):
        for a in range(3):
            for part in range(2):
                edges.put(
                    base + part * 6 + s * 3 + a,
                    for_earlier[s][a][part] * at_first,
                    for_later[s][a][part] * at_last,
                )


def scaled_half(half, factor):
    return [[(v[0] * factor, v[1] * factor) for v in r] for r in half]


def add_half(x, y):
    return [[plus(x[s][a], y[s][a], 0) for a in range(3)] for s in range(2)]


def hop_at(field, links, time, parity, dagger, high=None, low=None):
    forward, backward = (1, -1) if dagger else (-1, 1)
    total = [[None] * 3 for _ in range(4)]
    own = load_spinor(field, time)
    for hop_dir in range(3):
        half = shift(project(own, hop_dir, forward), hop_dir, time, parity, 1)
        half = link_mul(link_at(links, parity, hop_dir, time), half)
        expand_onto(total, half, hop_dir, forward)
        half = link_mul_adj(
            link_at(links, 1 - parity, hop_dir, time), project(own, hop_dir, backward)
        )
        expand_onto(total, shift(half, hop_dir, time, parity, -1), hop_dir, backward)
    if time == 0:
        half = project(load_spinor(field, 1), 3, forward)
        expand_onto(total, link_mul(link_at(links, parity, 3, 0), half), 3, forward)
        if low is not None:
            expand_onto(total, low, 3, backward)
    else:
        half = project(load_spinor(field, 0), 3, backward)
        expand_onto(total, link_mul_adj(link_at(links, 1 - parity, 3, 0), half), 3, backward)
        if high is not None:
            expand_onto(total, link_mul(link_at(links, parity, 3, 1), high), 3, forward)
    return total


def block_at(clover, chiral, time):
    diagonal = [clover[chiral, 0, i, i, time].astype(F32) for i in range(6)]
    upper = {
        (i, j): (
            clover[chiral, 0, i, j, time].astype(F32),
            clover[chiral, 1, i, j, time].astype(F32),
        )
        for i, j in PAIRS
    }
    return diagonal, upper


def block_packed(row):
    diagonal = [row(i) for i in range(6)]
    upper = {pair: (row(6 + 2 * n), row(7 + 2 * n)) for n, pair in enumerate(PAIRS)}
    return diagonal, upper


def block_mul(block, half):
    diagonal, upper = block
    flat = half[0] + half[1]
    out = [(diagonal[i] * flat[i][0], diagonal[i] * flat[i][1]) for i in range(6)]
    for i, j in PAIRS:
        out[i] = plus(out[i], mul(upper[i, j], flat[j]), 0)
        out[j] = plus(out[j], mul_conj(upper[i, j], flat[i]), 0)
    return [out[:3], out[3:]]


def clover_at(clover, spinor, time):
    return block_mul(block_at(clover, 0, time), spinor[:2]) + block_mul(
        block_at(clover, 1, time), spinor[2:]
    )


def edge_signs():
    position = lax.axis_index("lat")
    last = lax.axis_size("lat") - 1
    at_first = jnp.where(position == 0, -1.0, 1.0).astype(F32)
    at_last = jnp.where(position == last, -1.0, 1.0).astype(F32)
    return at_first, at_last


def begin_schur(vector, links, odd_inverse, dagger, partial, sent):
    forward, backward = (1, -1) if dagger else (-1, 1)
    for time in range(2):
        store_spinor(
            partial, clover_at(odd_inverse, hop_at(vector, links, time, 1, dagger), time), time
        )
    for base, field, parity in ((0, vector, 0), (12, partial, 1)):
        earlier = project(load_spinor(field, 0), 3, forward)
        later = project(load_spinor(field, 1), 3, backward)
        store_halves(sent, earlier, link_mul_adj(link_at(links, parity, 3, 1), later), base)


def end_schur(
    vector, partial, sent, got, around, links, even, odd_inverse, dagger, odd_field, result
):
    forward, backward = (1, -1) if dagger else (-1, 1)
    at_first, at_last = edge_signs()
    for time in range(2):
        if time == 0:
            half, sign = load_half(got.low), backward
        else:
            half = link_mul(link_at(links, 1, 3, 1), load_half(got.high))
            sign = forward
        own = load_spinor(partial, time)
        top = block_mul(block_at(odd_inverse, 0, time), half)
        bottom = block_mul(block_at(odd_inverse, 1, time), half)
        whole = [[plus(own[s][a], top[s][a], 0) for a in range(3)] for s in range(2)] + [
            [plus(own[2 + s][a], bottom[s][a], 0 if sign > 0 else 2) for a in range(3)]
            for s in range(2)
        ]
        store_spinor(odd_field, whole, time)
    back = block_mul(block_packed(around.high), load_half(sent.high))
    high = add_half(load_half(got.high, 12), scaled_half(back, at_last))
    back = block_mul(block_packed(around.low), load_half(sent.low))
    low = add_half(load_half(got.low, 12), scaled_half(back, at_first))
    for time in range(2):
        returned = hop_at(odd_field, links, time, 0, dagger, high, low)
        direct = clover_at(even, load_spinor(vector, time), time)
        factor = KAPPA * KAPPA
        store_spinor(
            result,
            [
                [
                    (
                        direct[s][a][0] - factor * returned[s][a][0],
                        direct[s][a][1] - factor * returned[s][a][1],
                    )
                    for a in range(3)
                ]
                for s in range(4)
            ],
            time,
        )


def around_kernel(links, odd_inverse, _, far, near):
    blocks = []
    for time in range(2):
        diagonal0, upper0 = block_at(odd_inverse, 0, time)
        diagonal1, upper1 = block_at(odd_inverse, 1, time)
        blocks.append(
            (
                [x - y for x, y in zip(diagonal0, diagonal1)],
                {pair: plus(upper0[pair], upper1[pair], 2) for pair in PAIRS},
            )
        )
    diagonal, upper = blocks[0]
    earlier = diagonal + [part for pair in PAIRS for part in upper[pair]]
    later = [None] * 36
    diagonal, upper = blocks[1]

    def entry(i, j):
        if i == j:
            return (diagonal[i], jnp.zeros_like(diagonal[i]))
        if i < j:
            return upper[i, j]
        value = upper[j, i]
        return (value[0], -value[1])

    link = link_at(links, 1, 3, 1)
    for s0, s1 in ((0, 0), (0, 1), (1, 1)):
        right = [[None] * 3 for _ in range(3)]
        for a in range(3):
            for b in range(3):
                total = mul(entry(s0 * 3 + a, s1 * 3), link[0][b])
                for c in (1, 2):
                    total = plus(total, mul(entry(s0 * 3 + a, s1 * 3 + c), link[c][b]), 0)
                right[a][b] = total
        for a in range(3):
            for b in range(3):
                if s0 == s1 and a > b:
                    continue
                total = mul_conj(link[0][a], right[0][b])
                for c in (1, 2):
                    total = plus(total, mul_conj(link[c][a], right[c][b]), 0)
                i, j = s0 * 3 + a, s1 * 3 + b
                if i == j:
                    later[i] = total[0]
                else:
                    n = PAIRS.index((i, j))
                    later[6 + 2 * n], later[7 + 2 * n] = total
    edges = Swapped(far, near)
    for n in range(36):
        edges.put(n, earlier[n], later[n])


def pack_kernel(noise, colours, out):
    out[:48] = noise[...]
    out[48:] = colours[...].astype(F32)


def start_kernel(probe_rows, gathered, links, odd_inverse, probes, turned, rhs, far, near, raw):
    for q in range(4):
        raw[:, :, 2 * q : 2 * q + 2, :] = gathered[q]
    probe_row = probe_rows[lax.axis_index("sub")]
    for parity in range(2):
        for time in range(2):
            masked = jnp.bitwise_and(raw[48 + parity, time].astype(jnp.int32), probe_row)
            masked = jnp.bitwise_xor(masked, jnp.right_shift(masked, 2))
            masked = jnp.bitwise_xor(masked, jnp.right_shift(masked, 1))
            sign = (1 - 2 * jnp.bitwise_and(masked, 1)).astype(F32)
            for n in range(24):
                probes[parity, time, n] = raw[parity * 24 + n, time] * sign
    for time in range(2):
        store_spinor(turned, clover_at(odd_inverse, load_spinor(probes, 1, time), time), time)
    for time in range(2):
        total = hop_at(turned, links, time, 0, False)
        own = load_spinor(probes, 0, time)
        store_spinor(
            rhs,
            [
                [
                    (own[s][a][0] + KAPPA * total[s][a][0], own[s][a][1] + KAPPA * total[s][a][1])
                    for a in range(3)
                ]
                for s in range(4)
            ],
            time,
        )
    half = link_mul_adj(link_at(links, 1, 3, 1), project(load_spinor(turned, 1), 3, 1))
    store_halves(Swapped(far, near), project(load_spinor(turned, 0), 3, -1), half, 0)


def rhs_kernel(partial, got_far, got_near, links, odd_inverse, rhs, odd, far, near):
    got = Swapped(got_far, got_near)
    half = scaled_half(load_half(got.low), KAPPA)
    store_spinor(rhs, expand_onto(load_spinor(partial, 0), half, 3, 1), 0)
    half = scaled_half(link_mul(link_at(links, 0, 3, 1), load_half(got.high)), KAPPA)
    store_spinor(rhs, expand_onto(load_spinor(partial, 1), half, 3, -1), 1)
    begin_schur(rhs, links, odd_inverse, True, odd, Swapped(far, near))


def step_kernel(
    dagger,
    vector, partial, sent_far, sent_near, got_far, got_near, around_far, around_near,
    links, even, odd_inverse,
    result, odd, far, near, odd_field,
):
    end_schur(
        vector, partial, Swapped(sent_far, sent_near), Swapped(got_far, got_near),
        Swapped(around_far, around_near), links, even, odd_inverse, dagger, odd_field, result,
    )
    begin_schur(result, links, odd_inverse, not dagger, odd, Swapped(far, near))


def column_sum(left, right):
    total = None
    for time in range(2):
        for n in range(24):
            term = left(time, n) * right(time, n)
            total = term if total is None else total + term
    return jnp.sum(total, axis=0, keepdims=True)


def last_kernel(
    vector, partial, sent_far, sent_near, got_far, got_near, around_far, around_near,
    links, even, odd_inverse, first, image,
    odd_field, sums, result,
):
    end_schur(
        vector, partial, Swapped(sent_far, sent_near), Swapped(got_far, got_near),
        Swapped(around_far, around_near), links, even, odd_inverse, False, odd_field, result,
    )
    first_at = lambda time, n: first[time, n]
    image_at = lambda time, n: image[time, n]
    vector_at = lambda time, n: vector[time, n]
    norm = column_sum(first_at, first_at)
    image_norm = column_sum(image_at, image_at)
    norm_all = jnp.sum(norm, axis=1, keepdims=True)
    about = jnp.sum(image_norm, axis=1, keepdims=True) / jnp.where(norm_all > 0, norm_all, 1.0)
    about = jnp.broadcast_to(about, (1, 128))
    about_full = jnp.broadcast_to(about, (8, 128))
    rest_at = lambda time, n: vector[time, n] - about_full * first[time, n]
    image_rest_at = lambda time, n: result[time, n] - about_full * image[time, n]
    rows = [
        norm,
        column_sum(first_at, vector_at),
        about,
        column_sum(rest_at, rest_at),
        column_sum(rest_at, first_at),
        column_sum(image_rest_at, image_rest_at),
        column_sum(image_rest_at, image_at),
        image_norm,
    ]
    block = jnp.concatenate(rows, axis=0)
    for n in range(sums.shape[0]):
        sums[n] = block


def trace_kernel(sums, probes, turned, first, first_odd, second, second_odd, *outs):
    core, chip = lax.rem(lax.axis_index("sub"), 2), lax.axis_index("sub") // 2
    whole = lambda x: jnp.sum(jnp.sum(x, axis=0, keepdims=True), axis=1, keepdims=True)
    row = [sums[:, n, :] for n in range(8)]
    norm, crossed, about, rest, rest_first, image_rest, image_cross, image_norm = row
    norm_all = whole(norm)
    inverse = whole(crossed) / norm_all
    alpha = norm_all / whole(crossed)
    off = about - inverse
    norm_next = alpha * alpha * whole(rest + 2.0 * off * rest_first + off * off * norm)
    beta = norm_next / norm_all
    off = about - (1.0 + beta) / alpha
    curved = alpha * alpha * whole(
        image_rest + 2.0 * off * image_cross + off * off * image_norm
    )
    alpha_next = norm_next / curved
    alpha = jnp.broadcast_to(alpha, (8, 128))
    alpha_next = jnp.broadcast_to(alpha_next, (8, 128))
    beta = jnp.broadcast_to(beta, (8, 128))
    for time in range(2):
        for parity in range(2):
            values = []
            for n in range(24):
                if parity == 0:
                    base, other = first[time, n], second[time, n]
                else:
                    base, other = first_odd[time, n], second_odd[time, n]
                search = (base - alpha * other) + beta * base
                value = alpha * base + alpha_next * search
                if parity == 1:
                    value = turned[time, n] + KAPPA * value
                values.append(value)
            right = [
                [(values[s * 3 + a], values[12 + s * 3 + a]) for a in range(3)] for s in range(4)
            ]
            left = load_spinor(probes, parity, time)

            def dot(s, r):
                total = mul_conj(left[s][0], right[r][0])
                for a in (1, 2):
                    total = plus(total, mul_conj(left[s][a], right[r][a]), 0)
                return total

            up = [[dot(s, 2 + r) for r in range(2)] for s in range(2)]
            down = [[dot(2 + s, r) for r in range(2)] for s in range(2)]
            x_sum = plus(plus(down[0][1], down[1][0], 0), plus(up[0][1], up[1][0], 0), 2)
            y_sum = plus(plus(down[0][1], down[1][0], 2), plus(up[0][1], up[1][0], 2), 2)
            z_sum = plus(plus(down[0][0], down[1][1], 2), plus(up[0][0], up[1][1], 2), 2)
            t_sum = plus(plus(down[0][0], down[1][1], 0), plus(up[0][0], up[1][1], 0), 0)
            columns = ((-x_sum[1], x_sum[0]), y_sum, (-z_sum[1], z_sum[0]), t_sum)
            for hop_dir in range(4):
                for part in range(2):
                    value = columns[hop_dir][part]
                    place = parity * 8 + part * 4 + hop_dir
                    quarters = [value[2 * q : 2 * q + 2] for q in range(4)]
                    for low in range(2):
                        halves = [
                            lax.select(core != low, quarters[2 * n + 1], quarters[2 * n])
                            for n in range(2)
                        ]
                        for high in range(2):
                            outs[2 * high + low][place, time] = lax.select(
                                chip != high, halves[1], halves[0]
                            )


VMEM = pl.BlockSpec(memory_space=pltpu.VMEM)
SMEM = pl.BlockSpec(memory_space=pltpu.SMEM)
ANY = pl.BlockSpec(memory_space=pl.ANY)


def call(kernel, name, shapes, scalars, arrays, scratch=(), outside=()):
    return pl.pallas_call(
        kernel,
        out_shape=tuple(jax.ShapeDtypeStruct(s, F32) for s in shapes),
        in_specs=[SMEM] * len(scalars)
        + [ANY if n in outside else VMEM for n in range(len(arrays))],
        out_specs=tuple(VMEM for _ in shapes),
        scratch_shapes=[pltpu.VMEM(s, F32) for s in scratch],
        compiler_params=pltpu.CompilerParams(vmem_limit_bytes=16 * 1024 * 1024),
        name=name,
    )(*scalars, *arrays)


FIELD = (2, 24, 8, 128)
EDGE = (24, 8, 128)


def swap(far, near):
    length = lax.axis_size("lat")
    place = range(length)
    return (
        lax.ppermute(far, "lat", [(i, (i + (1 if i % 2 else -1)) % length) for i in place]),
        lax.ppermute(near, "lat", [(i, i ^ 1) for i in place]),
    )


def whole(noise, colours, probe_rows, links, even, odd_inverse):
    (own,) = call(
        pack_kernel,
        "pack",
        ((50,) + noise.shape[4:],),
        (),
        (noise.reshape((48,) + noise.shape[4:]), colours),
    )
    gathered = lax.all_gather(own, "sub")
    probes, turned, partial, *sent = call(
        start_kernel,
        "start",
        ((2,) + FIELD, FIELD, FIELD, (12, 8, 128), (12, 8, 128)),
        (probe_rows,),
        (gathered, links, odd_inverse),
        ((50, 2, 8, 128),),
    )
    got = swap(*sent)
    around = swap(
        *call(
            around_kernel,
            "around",
            ((36, 8, 128),) * 2,
            (),
            (links, odd_inverse, turned),
            (),
            (2,),
        )
    )
    vector, odd, *sent = call(
        rhs_kernel, "rhs", (FIELD, FIELD, EDGE, EDGE), (), (partial, *got, links, odd_inverse)
    )
    kept = []
    for step in range(3):
        got = swap(*sent)
        arrays = (vector, odd, *sent, *got, *around, links, even, odd_inverse)
        keep = step == 1
        vector, odd, *sent = call(
            functools.partial(step_kernel, step % 2 == 0),
            "step%d" % step,
            (FIELD, FIELD, EDGE, EDGE) + (FIELD,) * keep,
            (),
            arrays,
            () if keep else (FIELD,),
        )
        if keep:
            first_odd = sent.pop()
        kept.append(vector)
    first, image, second = kept
    got = swap(*sent)
    second_odd, sums = call(
        last_kernel,
        "last",
        (FIELD, (lax.axis_size("lat"), 8, 128)),
        (),
        (second, odd, *sent, *got, *around, links, even, odd_inverse, first, image),
        (FIELD,),
    )
    sums = lax.all_to_all(sums, "lat", 0, 0, tiled=True)
    traces = call(
        trace_kernel,
        "trace",
        ((16, 2, 2, 128),) * 4,
        (),
        (sums, probes, turned, first, first_odd, second, second_odd),
    )
    total = traces[0]
    for n in (3, 2, 1):
        total = total + lax.ppermute(traces[n], "sub", [(i, i ^ n) for i in range(4)])
    return total.reshape(2, 2, 4, 2, 2, 128)


def solution(mesh):
    placed = (
        P(None, None, None, None, "lat", "sub", None),
        P(None, "lat", "sub", None),
        P(),
        P(None, None, None, None, None, "lat", None, None),
        P(None, None, None, None, "lat", None, None),
        P(None, None, None, None, "lat", None, None),
    )
    return jax.shard_map(
        whole,
        mesh=mesh,
        in_specs=placed,
        out_specs=P(None, None, None, "lat", "sub", None),
        check_vma=False,
    )
```

```python
import functools

import jax
import jax.numpy as jnp
from jax import lax
from jax.experimental import pallas as pl
from jax.experimental.pallas import tpu as pltpu
from jax.sharding import PartitionSpec as P

KAPPA = 0.135
F32 = jnp.float32

TURN = (
    ((1, 1), (0, 1)),
    ((1, 0), (0, 2)),
    ((0, 1), (1, 3)),
    ((0, 0), (1, 0)),
)
PAIRS = tuple((i, j) for i in range(6) for j in range(i + 1, 6))


def plus(x, y, power):
    power = power % 4
    if power == 0:
        return (x[0] + y[0], x[1] + y[1])
    if power == 1:
        return (x[0] - y[1], x[1] + y[0])
    if power == 2:
        return (x[0] - y[0], x[1] - y[1])
    return (x[0] + y[1], x[1] - y[0])


def mul(x, y):
    return (x[0] * y[0] - x[1] * y[1], x[0] * y[1] + x[1] * y[0])


def mul_conj(x, y):
    return (x[0] * y[0] + x[1] * y[1], x[0] * y[1] - x[1] * y[0])


def project(spinor, hop_dir, sign):
    if hop_dir == 3:
        extra = 0 if sign > 0 else 2
    else:
        extra = 2 if sign > 0 else 0
    return [
        [
            plus(spinor[s][a], spinor[2 + TURN[hop_dir][s][0]][a], TURN[hop_dir][s][1] + extra)
            for a in range(3)
        ]
        for s in range(2)
    ]


def expand_onto(total, half, hop_dir, sign):
    extra = 0 if sign > 0 else 2
    for s in range(2):
        source, power = TURN[hop_dir][s]
        for a in range(3):
            total[s][a] = half[s][a] if total[s][a] is None else plus(total[s][a], half[s][a], 0)
            if total[2 + s][a] is None:
                zero = jnp.zeros_like(half[source][a][0])
                total[2 + s][a] = plus((zero, zero), half[source][a], power + extra)
            else:
                total[2 + s][a] = plus(total[2 + s][a], half[source][a], power + extra)
    return total


def link_at(links, parity, hop_dir, time):
    return [
        [
            (
                links[parity, hop_dir, 0, i, j, time].astype(F32),
                links[parity, hop_dir, 1, i, j, time].astype(F32),
            )
            for j in range(3)
        ]
        for i in range(3)
    ]


def link_mul(link, half):
    out = []
    for s in range(2):
        row = []
        for i in range(3):
            total = mul(link[i][0], half[s][0])
            for j in (1, 2):
                total = plus(total, mul(link[i][j], half[s][j]), 0)
            row.append(total)
        out.append(row)
    return out


def link_mul_adj(link, half):
    out = []
    for s in range(2):
        row = []
        for i in range(3):
            total = mul_conj(link[0][i], half[s][0])
            for j in (1, 2):
                total = plus(total, mul_conj(link[j][i], half[s][j]), 0)
            row.append(total)
        out.append(row)
    return out


def shift_x(half, time, parity, offset):
    shape = (8, 128)
    depth = lax.broadcasted_iota(jnp.int32, shape, 0)
    lane = lax.broadcasted_iota(jnp.int32, shape, 1)
    row = (depth + lane // 4 + (time + parity)) % 2
    wanted = 1 if offset > 0 else 0
    moved = (lane // 4) * 4 + (lane + offset) % 4
    index = jnp.where(row == wanted, moved, lane)
    pick = lambda v: jnp.take_along_axis(v, index, axis=1, mode="promise_in_bounds")
    return [[(pick(v[0]), pick(v[1])) for v in r] for r in half]


def shift(half, hop_dir, time, parity, offset):
    if hop_dir == 0:
        return shift_x(half, time, parity, offset)
    if hop_dir == 1:
        pick = lambda v: pltpu.roll(v, (-4 * offset) % 128, 1)
    else:
        pick = lambda v: pltpu.roll(v, (-offset) % 8, 0)
    return [[(pick(v[0]), pick(v[1])) for v in r] for r in half]


def load_spinor(ref, *lead):
    return [
        [(ref[(*lead, s * 3 + a)], ref[(*lead, 12 + s * 3 + a)]) for a in range(3)]
        for s in range(4)
    ]


def store_spinor(ref, spinor, *lead):
    for s in range(4):
        for a in range(3):
            ref[(*lead, s * 3 + a)] = spinor[s][a][0]
            ref[(*lead, 12 + s * 3 + a)] = spinor[s][a][1]


class Swapped:

    def __init__(self, far, near):
        self.far, self.near = far, near
        self.odd = lax.rem(lax.axis_index("lat"), 2) == 1

    def high(self, n):
        return lax.select(self.odd, self.far[n], self.near[n])

    def low(self, n):
        return lax.select(self.odd, self.near[n], self.far[n])

    def put(self, n, for_earlier, for_later):
        self.far[n] = lax.select(self.odd, for_later, for_earlier)
        self.near[n] = lax.select(self.odd, for_earlier, for_later)


def load_half(row, base=0):
    return [
        [(row(base + s * 3 + a), row(base + 6 + s * 3 + a)) for a in range(3)] for s in range(2)
    ]


def store_halves(edges, for_earlier, for_later, base):
    at_first, at_last = edge_signs()
    for s in range(2):
        for a in range(3):
            for part in range(2):
                edges.put(
                    base + part * 6 + s * 3 + a,
                    for_earlier[s][a][part] * at_first,
                    for_later[s][a][part] * at_last,
                )


def scaled_half(half, factor):
    return [[(v[0] * factor, v[1] * factor) for v in r] for r in half]


def add_half(x, y):
    return [[plus(x[s][a], y[s][a], 0) for a in range(3)] for s in range(2)]


def hop_at(field, links, time, parity, dagger, high=None, low=None):
    forward, backward = (1, -1) if dagger else (-1, 1)
    total = [[None] * 3 for _ in range(4)]
    own = load_spinor(field, time)
    for hop_dir in range(3):
        half = shift(project(own, hop_dir, forward), hop_dir, time, parity, 1)
        half = link_mul(link_at(links, parity, hop_dir, time), half)
        expand_onto(total, half, hop_dir, forward)
        half = link_mul_adj(
            link_at(links, 1 - parity, hop_dir, time), project(own, hop_dir, backward)
        )
        expand_onto(total, shift(half, hop_dir, time, parity, -1), hop_dir, backward)
    if time == 0:
        half = project(load_spinor(field, 1), 3, forward)
        expand_onto(total, link_mul(link_at(links, parity, 3, 0), half), 3, forward)
        if low is not None:
            expand_onto(total, low, 3, backward)
    else:
        half = project(load_spinor(field, 0), 3, backward)
        expand_onto(total, link_mul_adj(link_at(links, 1 - parity, 3, 0), half), 3, backward)
        if high is not None:
            expand_onto(total, link_mul(link_at(links, parity, 3, 1), high), 3, forward)
    return total


def block_at(clover, chiral, time):
    diagonal = [clover[chiral, 0, i, i, time].astype(F32) for i in range(6)]
    upper = {
        (i, j): (
            clover[chiral, 0, i, j, time].astype(F32),
            clover[chiral, 1, i, j, time].astype(F32),
        )
        for i, j in PAIRS
    }
    return diagonal, upper


def block_packed(row):
    diagonal = [row(i) for i in range(6)]
    upper = {pair: (row(6 + 2 * n), row(7 + 2 * n)) for n, pair in enumerate(PAIRS)}
    return diagonal, upper


def block_mul(block, half):
    diagonal, upper = block
    flat = half[0] + half[1]
    out = [(diagonal[i] * flat[i][0], diagonal[i] * flat[i][1]) for i in range(6)]
    for i, j in PAIRS:
        out[i] = plus(out[i], mul(upper[i, j], flat[j]), 0)
        out[j] = plus(out[j], mul_conj(upper[i, j], flat[i]), 0)
    return [out[:3], out[3:]]


def clover_at(clover, spinor, time):
    return block_mul(block_at(clover, 0, time), spinor[:2]) + block_mul(
        block_at(clover, 1, time), spinor[2:]
    )


def edge_signs():
    position = lax.axis_index("lat")
    last = lax.axis_size("lat") - 1
    at_first = jnp.where(position == 0, -1.0, 1.0).astype(F32)
    at_last = jnp.where(position == last, -1.0, 1.0).astype(F32)
    return at_first, at_last


def begin_schur(vector, links, odd_inverse, dagger, partial, sent):
    forward, backward = (1, -1) if dagger else (-1, 1)
    for time in range(2):
        store_spinor(
            partial, clover_at(odd_inverse, hop_at(vector, links, time, 1, dagger), time), time
        )
    for base, field, parity in ((0, vector, 0), (12, partial, 1)):
        earlier = project(load_spinor(field, 0), 3, forward)
        later = project(load_spinor(field, 1), 3, backward)
        store_halves(sent, earlier, link_mul_adj(link_at(links, parity, 3, 1), later), base)


def end_schur(
    direct, partial, sent, got, around, links, odd_inverse, dagger, odd_field, result
):
    forward, backward = (1, -1) if dagger else (-1, 1)
    at_first, at_last = edge_signs()
    for time in range(2):
        if time == 0:
            half, sign = load_half(got.low), backward
        else:
            half = link_mul(link_at(links, 1, 3, 1), load_half(got.high))
            sign = forward
        own = load_spinor(partial, time)
        top = block_mul(block_at(odd_inverse, 0, time), half)
        bottom = block_mul(block_at(odd_inverse, 1, time), half)
        whole = [[plus(own[s][a], top[s][a], 0) for a in range(3)] for s in range(2)] + [
            [plus(own[2 + s][a], bottom[s][a], 0 if sign > 0 else 2) for a in range(3)]
            for s in range(2)
        ]
        store_spinor(odd_field, whole, time)
    back = block_mul(block_packed(around.high), load_half(sent.high))
    high = add_half(load_half(got.high, 12), scaled_half(back, at_last))
    back = block_mul(block_packed(around.low), load_half(sent.low))
    low = add_half(load_half(got.low, 12), scaled_half(back, at_first))
    for time in range(2):
        returned = hop_at(odd_field, links, time, 0, dagger, high, low)
        own = load_spinor(direct, time)
        factor = KAPPA * KAPPA
        store_spinor(
            result,
            [
                [
                    (
                        own[s][a][0] - factor * returned[s][a][0],
                        own[s][a][1] - factor * returned[s][a][1],
                    )
                    for a in range(3)
                ]
                for s in range(4)
            ],
            time,
        )


def around_kernel(links, odd_inverse, _, far, near):
    blocks = []
    for time in range(2):
        diagonal0, upper0 = block_at(odd_inverse, 0, time)
        diagonal1, upper1 = block_at(odd_inverse, 1, time)
        blocks.append(
            (
                [x - y for x, y in zip(diagonal0, diagonal1)],
                {pair: plus(upper0[pair], upper1[pair], 2) for pair in PAIRS},
            )
        )
    diagonal, upper = blocks[0]
    earlier = diagonal + [part for pair in PAIRS for part in upper[pair]]
    later = [None] * 36
    diagonal, upper = blocks[1]

    def entry(i, j):
        if i == j:
            return (diagonal[i], jnp.zeros_like(diagonal[i]))
        if i < j:
            return upper[i, j]
        value = upper[j, i]
        return (value[0], -value[1])

    link = link_at(links, 1, 3, 1)
    for s0, s1 in ((0, 0), (0, 1), (1, 1)):
        right = [[None] * 3 for _ in range(3)]
        for a in range(3):
            for b in range(3):
                total = mul(entry(s0 * 3 + a, s1 * 3), link[0][b])
                for c in (1, 2):
                    total = plus(total, mul(entry(s0 * 3 + a, s1 * 3 + c), link[c][b]), 0)
                right[a][b] = total
        for a in range(3):
            for b in range(3):
                if s0 == s1 and a > b:
                    continue
                total = mul_conj(link[0][a], right[0][b])
                for c in (1, 2):
                    total = plus(total, mul_conj(link[c][a], right[c][b]), 0)
                i, j = s0 * 3 + a, s1 * 3 + b
                if i == j:
                    later[i] = total[0]
                else:
                    n = PAIRS.index((i, j))
                    later[6 + 2 * n], later[7 + 2 * n] = total
    edges = Swapped(far, near)
    for n in range(36):
        edges.put(n, earlier[n], later[n])


def pack_kernel(noise, colours, out):
    out[:48] = noise[...]
    out[48:] = colours[...].astype(F32)


def unpack_probes(probe_rows, gathered, raw, parity, probes):
    probe_row = probe_rows[lax.axis_index("sub")]
    for q in range(4):
        raw[:24, :, 2 * q : 2 * q + 2, :] = gathered[q, 24 * parity : 24 * parity + 24]
        raw[24, :, 2 * q : 2 * q + 2, :] = gathered[q, 48 + parity]
    for time in range(2):
        masked = jnp.bitwise_and(raw[24, time].astype(jnp.int32), probe_row)
        masked = jnp.bitwise_xor(masked, jnp.right_shift(masked, 2))
        masked = jnp.bitwise_xor(masked, jnp.right_shift(masked, 1))
        sign = (1 - 2 * jnp.bitwise_and(masked, 1)).astype(F32)
        for n in range(24):
            probes[time, n] = raw[n, time] * sign


def start_kernel(probe_rows, gathered, time_link, odd_inverse, probes, turned, far, near, raw):
    unpack_probes(probe_rows, gathered, raw, 1, probes)
    for time in range(2):
        store_spinor(turned, clover_at(odd_inverse, load_spinor(probes, time), time), time)
    link = [
        [(time_link[0, i, j, 1].astype(F32), time_link[1, i, j, 1].astype(F32)) for j in range(3)]
        for i in range(3)
    ]
    half = link_mul_adj(link, project(load_spinor(turned, 1), 3, 1))
    store_halves(Swapped(far, near), project(load_spinor(turned, 0), 3, -1), half, 0)


def own_rhs_kernel(probe_rows, gathered, turned, links, probes, rhs, raw):
    unpack_probes(probe_rows, gathered, raw, 0, probes)
    for time in range(2):
        total = hop_at(turned, links, time, 0, False)
        own = load_spinor(probes, time)
        store_spinor(
            rhs,
            [
                [
                    (own[s][a][0] + KAPPA * total[s][a][0], own[s][a][1] + KAPPA * total[s][a][1])
                    for a in range(3)
                ]
                for s in range(4)
            ],
            time,
        )


def direct_kernel(vector, even, out):
    for time in range(2):
        store_spinor(out, clover_at(even, load_spinor(vector, time), time), time)


def rhs_kernel(partial, got_far, got_near, links, odd_inverse, rhs, odd, far, near):
    got = Swapped(got_far, got_near)
    half = scaled_half(load_half(got.low), KAPPA)
    store_spinor(rhs, expand_onto(load_spinor(partial, 0), half, 3, 1), 0)
    half = scaled_half(link_mul(link_at(links, 0, 3, 1), load_half(got.high)), KAPPA)
    store_spinor(rhs, expand_onto(load_spinor(partial, 1), half, 3, -1), 1)
    begin_schur(rhs, links, odd_inverse, True, odd, Swapped(far, near))


def step_kernel(
    dagger,
    direct, partial, sent_far, sent_near, got_far, got_near, around_far, around_near,
    links, odd_inverse,
    result, odd, far, near, odd_field,
):
    end_schur(
        direct, partial, Swapped(sent_far, sent_near), Swapped(got_far, got_near),
        Swapped(around_far, around_near), links, odd_inverse, dagger, odd_field, result,
    )
    begin_schur(result, links, odd_inverse, not dagger, odd, Swapped(far, near))


def column_sum(left, right):
    total = None
    for time in range(2):
        for n in range(24):
            term = left(time, n) * right(time, n)
            total = term if total is None else total + term
    return jnp.sum(total, axis=0, keepdims=True)


def traces_at(left, right):
    def dot(s, r):
        total = mul_conj(left[s][0], right[r][0])
        for a in (1, 2):
            total = plus(total, mul_conj(left[s][a], right[r][a]), 0)
        return total

    up = [[dot(s, 2 + r) for r in range(2)] for s in range(2)]
    down = [[dot(2 + s, r) for r in range(2)] for s in range(2)]
    x_sum = plus(plus(down[0][1], down[1][0], 0), plus(up[0][1], up[1][0], 0), 2)
    y_sum = plus(plus(down[0][1], down[1][0], 2), plus(up[0][1], up[1][0], 2), 2)
    z_sum = plus(plus(down[0][0], down[1][1], 2), plus(up[0][0], up[1][1], 2), 2)
    t_sum = plus(plus(down[0][0], down[1][1], 0), plus(up[0][0], up[1][1], 0), 0)
    columns = ((-x_sum[1], x_sum[0]), y_sum, (-z_sum[1], z_sum[0]), t_sum)
    return [columns[hop_dir][part] for part in range(2) for hop_dir in range(4)]


def store_traces(out, place, probes, field, time):
    for n, value in enumerate(traces_at(load_spinor(probes, time), load_spinor(field, time))):
        out[place, n, time] = value


def traces_kernel(probes_even, probes_odd, turned, first, first_odd, second, second_odd, out):
    for time in range(2):
        store_traces(out, 0, probes_even, first, time)
        store_traces(out, 1, probes_even, second, time)
        store_traces(out, 2, probes_odd, turned, time)
        store_traces(out, 3, probes_odd, first_odd, time)
        store_traces(out, 4, probes_odd, second_odd, time)


def in_lanes(row, values):
    lane = lax.broadcasted_iota(jnp.int32, (1, 128), 1)
    for n, value in values.items():
        value = jnp.broadcast_to(jnp.sum(value, axis=1, keepdims=True), (1, 128))
        row = jnp.where(lane == n, value, row)
    return row


def sums_kernel(first, image, vector, row, about):
    first_at = lambda time, n: first[time, n]
    image_at = lambda time, n: image[time, n]
    vector_at = lambda time, n: vector[time, n]
    whole = lambda x: jnp.sum(x, axis=1, keepdims=True)
    norm = column_sum(first_at, first_at)
    image_norm = column_sum(image_at, image_at)
    norm_all = whole(norm)
    shift_by = jnp.broadcast_to(
        whole(image_norm) / jnp.where(norm_all > 0, norm_all, 1.0), (8, 128)
    )
    about[...] = shift_by
    rest_at = lambda time, n: vector[time, n] - shift_by * first[time, n]
    lane = lax.broadcasted_iota(jnp.int32, (1, 128), 1)
    row[...] = in_lanes(
        jnp.where(lane == 2, shift_by[:1], 0.0),
        {
            0: norm,
            1: column_sum(first_at, vector_at),
            3: column_sum(rest_at, rest_at),
            4: column_sum(rest_at, first_at),
            7: image_norm,
        },
    )


def last_kernel(
    direct, partial, sent_far, sent_near, got_far, got_near, around_far, around_near,
    links, odd_inverse, image, row, about,
    odd_field, sums, result,
):
    end_schur(
        direct, partial, Swapped(sent_far, sent_near), Swapped(got_far, got_near),
        Swapped(around_far, around_near), links, odd_inverse, False, odd_field, result,
    )
    image_at = lambda time, n: image[time, n]
    rest_at = lambda time, n: result[time, n] - about[...] * image[time, n]
    sums[...] = jnp.broadcast_to(
        in_lanes(row[...], {5: column_sum(rest_at, rest_at), 6: column_sum(rest_at, image_at)}),
        sums.shape,
    )


def final_kernel(sums, own, *outs):
    core, chip = lax.rem(lax.axis_index("sub"), 2), lax.axis_index("sub") // 2
    table = sums[...]
    first_lane = lax.broadcasted_iota(jnp.int32, table.shape, 1) == 0
    norm, crossed, about, rest, rest_first, image_rest, image_cross, image_norm = [
        table if n == 0 else pltpu.roll(table, 128 - n, 1) for n in range(8)
    ]
    whole = lambda x: jnp.sum(
        jnp.sum(jnp.where(first_lane, x, 0.0), axis=0, keepdims=True), axis=1, keepdims=True
    )
    norm_all, crossed_all = whole(norm), whole(crossed)
    alpha = norm_all / crossed_all
    off = about - crossed_all / norm_all
    norm_next = alpha * alpha * whole(rest + 2.0 * off * rest_first + off * off * norm)
    beta = norm_next / norm_all
    off = about - (1.0 + beta) / alpha
    curved = alpha * alpha * whole(
        image_rest + 2.0 * off * image_cross + off * off * image_norm
    )
    alpha_next = norm_next / curved
    of_first = jnp.broadcast_to(alpha + alpha_next * (1.0 + beta), (8, 128))
    of_second = jnp.broadcast_to(-alpha * alpha_next, (8, 128))
    for time in range(2):
        for n in range(8):
            even = of_first * own[0, n, time] + of_second * own[1, n, time]
            odd = own[2, n, time] + KAPPA * (
                of_first * own[3, n, time] + of_second * own[4, n, time]
            )
            for place, value in ((n, even), (8 + n, odd)):
                quarters = [value[2 * q : 2 * q + 2] for q in range(4)]
                for low in range(2):
                    halves = [
                        lax.select(core != low, quarters[2 * q + 1], quarters[2 * q])
                        for q in range(2)
                    ]
                    for high in range(2):
                        outs[2 * high + low][place, time] = lax.select(
                            chip != high, halves[1], halves[0]
                        )


VMEM = pl.BlockSpec(memory_space=pltpu.VMEM)
SMEM = pl.BlockSpec(memory_space=pltpu.SMEM)
ANY = pl.BlockSpec(memory_space=pl.ANY)


def call(kernel, name, shapes, scalars, arrays, scratch=(), outside=()):
    return pl.pallas_call(
        kernel,
        out_shape=tuple(jax.ShapeDtypeStruct(s, F32) for s in shapes),
        in_specs=[SMEM] * len(scalars)
        + [ANY if n in outside else VMEM for n in range(len(arrays))],
        out_specs=tuple(VMEM for _ in shapes),
        scratch_shapes=[pltpu.VMEM(s, F32) for s in scratch],
        compiler_params=pltpu.CompilerParams(vmem_limit_bytes=16 * 1024 * 1024),
        name=name,
    )(*scalars, *arrays)


FIELD = (2, 24, 8, 128)
EDGE = (24, 8, 128)


def swap(far, near):
    length = lax.axis_size("lat")
    place = range(length)
    return (
        lax.ppermute(far, "lat", [(i, (i + (1 if i % 2 else -1)) % length) for i in place]),
        lax.ppermute(near, "lat", [(i, i ^ 1) for i in place]),
    )


def whole(noise, colours, probe_rows, links, even, odd_inverse):
    (own,) = call(
        pack_kernel,
        "pack",
        ((50,) + noise.shape[4:],),
        (),
        (noise.reshape((48,) + noise.shape[4:]), colours),
    )
    gathered = lax.all_gather(own, "sub")
    probes_odd, turned, *sent = call(
        start_kernel,
        "start",
        (FIELD, FIELD, (12, 8, 128), (12, 8, 128)),
        (probe_rows,),
        (gathered, links[1, 3], odd_inverse),
        ((25, 2, 8, 128),),
    )
    got = swap(*sent)
    probes_even, partial = call(
        own_rhs_kernel,
        "own_rhs",
        (FIELD, FIELD),
        (probe_rows,),
        (gathered, turned, links),
        ((25, 2, 8, 128),),
    )
    around = swap(
        *call(
            around_kernel,
            "around",
            ((36, 8, 128),) * 2,
            (),
            (links, odd_inverse, turned),
            (),
            (2,),
        )
    )
    vector, odd, *sent = call(
        rhs_kernel, "rhs", (FIELD, FIELD, EDGE, EDGE), (), (partial, *got, links, odd_inverse)
    )
    kept = []
    for step in range(3):
        got = swap(*sent)
        (direct,) = call(direct_kernel, "direct%d" % step, (FIELD,), (), (vector, even))
        arrays = (direct, odd, *sent, *got, *around, links, odd_inverse)
        keep = step == 1
        vector, odd, *sent = call(
            functools.partial(step_kernel, step % 2 == 0),
            "step%d" % step,
            (FIELD, FIELD, EDGE, EDGE) + (FIELD,) * keep,
            (),
            arrays,
            () if keep else (FIELD,),
        )
        if keep:
            first_odd = sent.pop()
        kept.append(vector)
    first, image, second = kept
    got = swap(*sent)
    (direct,) = call(direct_kernel, "direct3", (FIELD,), (), (second, even))
    row, about = call(
        sums_kernel, "sums", ((1, 128), (8, 128)), (), (first, image, second)
    )
    second_odd, sums = call(
        last_kernel,
        "last",
        (FIELD, (lax.axis_size("lat"), 128)),
        (),
        (direct, odd, *sent, *got, *around, links, odd_inverse, image, row, about),
        (FIELD,),
    )
    (own_traces,) = call(
        traces_kernel,
        "traces",
        ((5, 8, 2, 8, 128),),
        (),
        (probes_even, probes_odd, turned, first, first_odd, second, second_odd),
    )
    sums = lax.all_to_all(sums, "lat", 0, 0, tiled=True)
    traces = call(
        final_kernel, "final", ((16, 2, 2, 128),) * 4, (), (sums, own_traces)
    )
    total = traces[0]
    for n in (3, 2, 1):
        total = total + lax.ppermute(traces[n], "sub", [(i, i ^ n) for i in range(4)])
    return total.reshape(2, 2, 4, 2, 2, 128)


def solution(mesh):
    placed = (
        P(None, None, None, None, "lat", "sub", None),
        P(None, "lat", "sub", None),
        P(),
        P(None, None, None, None, None, "lat", None, None),
        P(None, None, None, None, "lat", None, None),
        P(None, None, None, None, "lat", None, None),
    )
    return jax.shard_map(
        whole,
        mesh=mesh,
        in_specs=placed,
        out_specs=P(None, None, None, "lat", "sub", None),
        check_vma=False,
    )
```

```python
import functools

import jax
import jax.numpy as jnp
from jax import lax
from jax.experimental import pallas as pl
from jax.experimental.pallas import tpu as pltpu
from jax.sharding import PartitionSpec as P

KAPPA = 0.135
F32 = jnp.float32

TURN = (
    ((1, 1), (0, 1)),
    ((1, 0), (0, 2)),
    ((0, 1), (1, 3)),
    ((0, 0), (1, 0)),
)
PAIRS = tuple((i, j) for i in range(6) for j in range(i + 1, 6))


def plus(x, y, power):
    power = power % 4
    if power == 0:
        return (x[0] + y[0], x[1] + y[1])
    if power == 1:
        return (x[0] - y[1], x[1] + y[0])
    if power == 2:
        return (x[0] - y[0], x[1] - y[1])
    return (x[0] + y[1], x[1] - y[0])


def mul(x, y):
    return (x[0] * y[0] - x[1] * y[1], x[0] * y[1] + x[1] * y[0])


def mul_conj(x, y):
    return (x[0] * y[0] + x[1] * y[1], x[0] * y[1] - x[1] * y[0])


def project(spinor, hop_dir, sign):
    if hop_dir == 3:
        extra = 0 if sign > 0 else 2
    else:
        extra = 2 if sign > 0 else 0
    return [
        [
            plus(spinor[s][a], spinor[2 + TURN[hop_dir][s][0]][a], TURN[hop_dir][s][1] + extra)
            for a in range(3)
        ]
        for s in range(2)
    ]


def expand_onto(total, half, hop_dir, sign):
    extra = 0 if sign > 0 else 2
    for s in range(2):
        source, power = TURN[hop_dir][s]
        for a in range(3):
            total[s][a] = half[s][a] if total[s][a] is None else plus(total[s][a], half[s][a], 0)
            if total[2 + s][a] is None:
                zero = jnp.zeros_like(half[source][a][0])
                total[2 + s][a] = plus((zero, zero), half[source][a], power + extra)
            else:
                total[2 + s][a] = plus(total[2 + s][a], half[source][a], power + extra)
    return total


def link_at(links, parity, hop_dir, time):
    return [
        [
            (
                links[parity, hop_dir, 0, i, j, time].astype(F32),
                links[parity, hop_dir, 1, i, j, time].astype(F32),
            )
            for j in range(3)
        ]
        for i in range(3)
    ]


def link_mul(link, half):
    out = []
    for s in range(2):
        row = []
        for i in range(3):
            total = mul(link[i][0], half[s][0])
            for j in (1, 2):
                total = plus(total, mul(link[i][j], half[s][j]), 0)
            row.append(total)
        out.append(row)
    return out


def link_mul_adj(link, half):
    out = []
    for s in range(2):
        row = []
        for i in range(3):
            total = mul_conj(link[0][i], half[s][0])
            for j in (1, 2):
                total = plus(total, mul_conj(link[j][i], half[s][j]), 0)
            row.append(total)
        out.append(row)
    return out


def shift_x(half, time, parity, offset):
    shape = (8, 128)
    depth = lax.broadcasted_iota(jnp.int32, shape, 0)
    lane = lax.broadcasted_iota(jnp.int32, shape, 1)
    row = (depth + lane // 4 + (time + parity)) % 2
    wanted = 1 if offset > 0 else 0
    moved = (lane // 4) * 4 + (lane + offset) % 4
    index = jnp.where(row == wanted, moved, lane)
    pick = lambda v: jnp.take_along_axis(v, index, axis=1, mode="promise_in_bounds")
    return [[(pick(v[0]), pick(v[1])) for v in r] for r in half]


def shift(half, hop_dir, time, parity, offset):
    if hop_dir == 0:
        return shift_x(half, time, parity, offset)
    if hop_dir == 1:
        pick = lambda v: pltpu.roll(v, (-4 * offset) % 128, 1)
    else:
        pick = lambda v: pltpu.roll(v, (-offset) % 8, 0)
    return [[(pick(v[0]), pick(v[1])) for v in r] for r in half]


def load_spinor(ref, *lead):
    return [
        [(ref[(*lead, s * 3 + a)], ref[(*lead, 12 + s * 3 + a)]) for a in range(3)]
        for s in range(4)
    ]


def store_spinor(ref, spinor, *lead):
    for s in range(4):
        for a in range(3):
            ref[(*lead, s * 3 + a)] = spinor[s][a][0]
            ref[(*lead, 12 + s * 3 + a)] = spinor[s][a][1]


class Swapped:

    def __init__(self, far, near):
        self.far, self.near = far, near
        self.odd = lax.rem(lax.axis_index("lat"), 2) == 1

    def high(self, n):
        return lax.select(self.odd, self.far[n], self.near[n])

    def low(self, n):
        return lax.select(self.odd, self.near[n], self.far[n])

    def put(self, n, for_earlier, for_later):
        self.far[n] = lax.select(self.odd, for_later, for_earlier)
        self.near[n] = lax.select(self.odd, for_earlier, for_later)


def load_half(row, base=0):
    return [
        [(row(base + s * 3 + a), row(base + 6 + s * 3 + a)) for a in range(3)] for s in range(2)
    ]


def store_halves(edges, for_earlier, for_later, base):
    at_first, at_last = edge_signs()
    for s in range(2):
        for a in range(3):
            for part in range(2):
                edges.put(
                    base + part * 6 + s * 3 + a,
                    for_earlier[s][a][part] * at_first,
                    for_later[s][a][part] * at_last,
                )


def scaled_half(half, factor):
    return [[(v[0] * factor, v[1] * factor) for v in r] for r in half]


def add_half(x, y):
    return [[plus(x[s][a], y[s][a], 0) for a in range(3)] for s in range(2)]


def hop_at(field, links, time, parity, dagger, high=None, low=None):
    forward, backward = (1, -1) if dagger else (-1, 1)
    total = [[None] * 3 for _ in range(4)]
    own = load_spinor(field, time)
    for hop_dir in range(3):
        half = shift(project(own, hop_dir, forward), hop_dir, time, parity, 1)
        half = link_mul(link_at(links, parity, hop_dir, time), half)
        expand_onto(total, half, hop_dir, forward)
        half = link_mul_adj(
            link_at(links, 1 - parity, hop_dir, time), project(own, hop_dir, backward)
        )
        expand_onto(total, shift(half, hop_dir, time, parity, -1), hop_dir, backward)
    if time == 0:
        half = project(load_spinor(field, 1), 3, forward)
        expand_onto(total, link_mul(link_at(links, parity, 3, 0), half), 3, forward)
        if low is not None:
            expand_onto(total, low, 3, backward)
    else:
        half = project(load_spinor(field, 0), 3, backward)
        expand_onto(total, link_mul_adj(link_at(links, 1 - parity, 3, 0), half), 3, backward)
        if high is not None:
            expand_onto(total, link_mul(link_at(links, parity, 3, 1), high), 3, forward)
    return total


def block_at(clover, chiral, time):
    diagonal = [clover[chiral, 0, i, i, time].astype(F32) for i in range(6)]
    upper = {
        (i, j): (
            clover[chiral, 0, i, j, time].astype(F32),
            clover[chiral, 1, i, j, time].astype(F32),
        )
        for i, j in PAIRS
    }
    return diagonal, upper


def block_packed(row):
    diagonal = [row(i) for i in range(6)]
    upper = {pair: (row(6 + 2 * n), row(7 + 2 * n)) for n, pair in enumerate(PAIRS)}
    return diagonal, upper


def block_mul(block, half):
    diagonal, upper = block
    flat = half[0] + half[1]
    out = [(diagonal[i] * flat[i][0], diagonal[i] * flat[i][1]) for i in range(6)]
    for i, j in PAIRS:
        out[i] = plus(out[i], mul(upper[i, j], flat[j]), 0)
        out[j] = plus(out[j], mul_conj(upper[i, j], flat[i]), 0)
    return [out[:3], out[3:]]


def clover_at(clover, spinor, time):
    return block_mul(block_at(clover, 0, time), spinor[:2]) + block_mul(
        block_at(clover, 1, time), spinor[2:]
    )


def edge_signs():
    position = lax.axis_index("lat")
    last = lax.axis_size("lat") - 1
    at_first = jnp.where(position == 0, -1.0, 1.0).astype(F32)
    at_last = jnp.where(position == last, -1.0, 1.0).astype(F32)
    return at_first, at_last


def begin_schur(vector, links, odd_inverse, dagger, partial, sent):
    forward, backward = (1, -1) if dagger else (-1, 1)
    for time in range(2):
        store_spinor(
            partial, clover_at(odd_inverse, hop_at(vector, links, time, 1, dagger), time), time
        )
    for base, field, parity in ((0, vector, 0), (12, partial, 1)):
        earlier = project(load_spinor(field, 0), 3, forward)
        later = project(load_spinor(field, 1), 3, backward)
        store_halves(sent, earlier, link_mul_adj(link_at(links, parity, 3, 1), later), base)


def end_schur(
    direct, partial, sent, got, around, links, odd_inverse, dagger, odd_field, result
):
    forward, backward = (1, -1) if dagger else (-1, 1)
    at_first, at_last = edge_signs()
    for time in range(2):
        if time == 0:
            half, sign = load_half(got.low), backward
        else:
            half = link_mul(link_at(links, 1, 3, 1), load_half(got.high))
            sign = forward
        own = load_spinor(partial, time)
        top = block_mul(block_at(odd_inverse, 0, time), half)
        bottom = block_mul(block_at(odd_inverse, 1, time), half)
        whole = [[plus(own[s][a], top[s][a], 0) for a in range(3)] for s in range(2)] + [
            [plus(own[2 + s][a], bottom[s][a], 0 if sign > 0 else 2) for a in range(3)]
            for s in range(2)
        ]
        store_spinor(odd_field, whole, time)
    back = block_mul(block_packed(around.high), load_half(sent.high))
    high = add_half(load_half(got.high, 12), scaled_half(back, at_last))
    back = block_mul(block_packed(around.low), load_half(sent.low))
    low = add_half(load_half(got.low, 12), scaled_half(back, at_first))
    for time in range(2):
        returned = hop_at(odd_field, links, time, 0, dagger, high, low)
        own = load_spinor(direct, time)
        factor = KAPPA * KAPPA
        store_spinor(
            result,
            [
                [
                    (
                        own[s][a][0] - factor * returned[s][a][0],
                        own[s][a][1] - factor * returned[s][a][1],
                    )
                    for a in range(3)
                ]
                for s in range(4)
            ],
            time,
        )


def around_kernel(links, odd_inverse, _, far, near):
    blocks = []
    for time in range(2):
        diagonal0, upper0 = block_at(odd_inverse, 0, time)
        diagonal1, upper1 = block_at(odd_inverse, 1, time)
        blocks.append(
            (
                [x - y for x, y in zip(diagonal0, diagonal1)],
                {pair: plus(upper0[pair], upper1[pair], 2) for pair in PAIRS},
            )
        )
    diagonal, upper = blocks[0]
    earlier = diagonal + [part for pair in PAIRS for part in upper[pair]]
    later = [None] * 36
    diagonal, upper = blocks[1]

    def entry(i, j):
        if i == j:
            return (diagonal[i], jnp.zeros_like(diagonal[i]))
        if i < j:
            return upper[i, j]
        value = upper[j, i]
        return (value[0], -value[1])

    link = link_at(links, 1, 3, 1)
    for s0, s1 in ((0, 0), (0, 1), (1, 1)):
        right = [[None] * 3 for _ in range(3)]
        for a in range(3):
            for b in range(3):
                total = mul(entry(s0 * 3 + a, s1 * 3), link[0][b])
                for c in (1, 2):
                    total = plus(total, mul(entry(s0 * 3 + a, s1 * 3 + c), link[c][b]), 0)
                right[a][b] = total
        for a in range(3):
            for b in range(3):
                if s0 == s1 and a > b:
                    continue
                total = mul_conj(link[0][a], right[0][b])
                for c in (1, 2):
                    total = plus(total, mul_conj(link[c][a], right[c][b]), 0)
                i, j = s0 * 3 + a, s1 * 3 + b
                if i == j:
                    later[i] = total[0]
                else:
                    n = PAIRS.index((i, j))
                    later[6 + 2 * n], later[7 + 2 * n] = total
    edges = Swapped(far, near)
    for n in range(36):
        edges.put(n, earlier[n], later[n])


def pack_kernel(noise, colours, out):
    out[:48] = noise[...]
    out[48:] = colours[...].astype(F32)


def unpack_probes(probe_rows, gathered, raw, parity, probes):
    upper = lax.axis_index("lat") // (lax.axis_size("lat") // 2)
    probe_row = probe_rows[jnp.bitwise_xor(lax.axis_index("sub"), 2 * upper)]
    for q in range(4):
        raw[:24, :, 2 * q : 2 * q + 2, :] = gathered[q, 24 * parity : 24 * parity + 24]
        raw[24, :, 2 * q : 2 * q + 2, :] = gathered[q, 48 + parity]
    for time in range(2):
        masked = jnp.bitwise_and(raw[24, time].astype(jnp.int32), probe_row)
        masked = jnp.bitwise_xor(masked, jnp.right_shift(masked, 2))
        masked = jnp.bitwise_xor(masked, jnp.right_shift(masked, 1))
        sign = (1 - 2 * jnp.bitwise_and(masked, 1)).astype(F32)
        for n in range(24):
            probes[time, n] = raw[n, time] * sign


def start_kernel(probe_rows, gathered, time_link, odd_inverse, probes, turned, far, near, raw):
    unpack_probes(probe_rows, gathered, raw, 1, probes)
    for time in range(2):
        store_spinor(turned, clover_at(odd_inverse, load_spinor(probes, time), time), time)
    link = [
        [(time_link[0, i, j, 1].astype(F32), time_link[1, i, j, 1].astype(F32)) for j in range(3)]
        for i in range(3)
    ]
    half = link_mul_adj(link, project(load_spinor(turned, 1), 3, 1))
    store_halves(Swapped(far, near), project(load_spinor(turned, 0), 3, -1), half, 0)


def own_rhs_kernel(probe_rows, gathered, turned, links, probes, rhs, raw):
    unpack_probes(probe_rows, gathered, raw, 0, probes)
    for time in range(2):
        total = hop_at(turned, links, time, 0, False)
        own = load_spinor(probes, time)
        store_spinor(
            rhs,
            [
                [
                    (own[s][a][0] + KAPPA * total[s][a][0], own[s][a][1] + KAPPA * total[s][a][1])
                    for a in range(3)
                ]
                for s in range(4)
            ],
            time,
        )


def direct_kernel(vector, even, out):
    for time in range(2):
        store_spinor(out, clover_at(even, load_spinor(vector, time), time), time)


def rhs_kernel(partial, got_far, got_near, links, odd_inverse, rhs, odd, far, near):
    got = Swapped(got_far, got_near)
    half = scaled_half(load_half(got.low), KAPPA)
    store_spinor(rhs, expand_onto(load_spinor(partial, 0), half, 3, 1), 0)
    half = scaled_half(link_mul(link_at(links, 0, 3, 1), load_half(got.high)), KAPPA)
    store_spinor(rhs, expand_onto(load_spinor(partial, 1), half, 3, -1), 1)
    begin_schur(rhs, links, odd_inverse, True, odd, Swapped(far, near))


def step_kernel(
    dagger,
    direct, partial, sent_far, sent_near, got_far, got_near, around_far, around_near,
    links, odd_inverse,
    result, odd, far, near, odd_field,
):
    end_schur(
        direct, partial, Swapped(sent_far, sent_near), Swapped(got_far, got_near),
        Swapped(around_far, around_near), links, odd_inverse, dagger, odd_field, result,
    )
    begin_schur(result, links, odd_inverse, not dagger, odd, Swapped(far, near))


def column_sum(left, right):
    total = None
    for time in range(2):
        for n in range(24):
            term = left(time, n) * right(time, n)
            total = term if total is None else total + term
    return jnp.sum(total, axis=0, keepdims=True)


def traces_at(left, right):
    def dot(s, r):
        total = mul_conj(left[s][0], right[r][0])
        for a in (1, 2):
            total = plus(total, mul_conj(left[s][a], right[r][a]), 0)
        return total

    up = [[dot(s, 2 + r) for r in range(2)] for s in range(2)]
    down = [[dot(2 + s, r) for r in range(2)] for s in range(2)]
    x_sum = plus(plus(down[0][1], down[1][0], 0), plus(up[0][1], up[1][0], 0), 2)
    y_sum = plus(plus(down[0][1], down[1][0], 2), plus(up[0][1], up[1][0], 2), 2)
    z_sum = plus(plus(down[0][0], down[1][1], 2), plus(up[0][0], up[1][1], 2), 2)
    t_sum = plus(plus(down[0][0], down[1][1], 0), plus(up[0][0], up[1][1], 0), 0)
    columns = ((-x_sum[1], x_sum[0]), y_sum, (-z_sum[1], z_sum[0]), t_sum)
    return [columns[hop_dir][part] for part in range(2) for hop_dir in range(4)]


def store_traces(out, place, probes, field, time):
    for n, value in enumerate(traces_at(load_spinor(probes, time), load_spinor(field, time))):
        out[place, n, time] = value


def traces_kernel(probes_even, probes_odd, turned, first, first_odd, second, second_odd, out):
    for time in range(2):
        store_traces(out, 0, probes_even, first, time)
        store_traces(out, 1, probes_even, second, time)
        store_traces(out, 2, probes_odd, turned, time)
        store_traces(out, 3, probes_odd, first_odd, time)
        store_traces(out, 4, probes_odd, second_odd, time)


def in_lanes(row, values):
    lane = lax.broadcasted_iota(jnp.int32, (1, 128), 1)
    for n, value in values.items():
        value = jnp.broadcast_to(jnp.sum(value, axis=1, keepdims=True), (1, 128))
        row = jnp.where(lane == n, value, row)
    return row


def sums_kernel(first, image, vector, row, about):
    first_at = lambda time, n: first[time, n]
    image_at = lambda time, n: image[time, n]
    vector_at = lambda time, n: vector[time, n]
    whole = lambda x: jnp.sum(x, axis=1, keepdims=True)
    norm = column_sum(first_at, first_at)
    image_norm = column_sum(image_at, image_at)
    norm_all = whole(norm)
    shift_by = jnp.broadcast_to(
        whole(image_norm) / jnp.where(norm_all > 0, norm_all, 1.0), (8, 128)
    )
    about[...] = shift_by
    rest_at = lambda time, n: vector[time, n] - shift_by * first[time, n]
    lane = lax.broadcasted_iota(jnp.int32, (1, 128), 1)
    row[...] = in_lanes(
        jnp.where(lane == 2, shift_by[:1], 0.0),
        {
            0: norm,
            1: column_sum(first_at, vector_at),
            3: column_sum(rest_at, rest_at),
            4: column_sum(rest_at, first_at),
            7: image_norm,
        },
    )


def last_kernel(
    direct, partial, sent_far, sent_near, got_far, got_near, around_far, around_near,
    links, odd_inverse, image, row, about,
    odd_field, sums, result,
):
    end_schur(
        direct, partial, Swapped(sent_far, sent_near), Swapped(got_far, got_near),
        Swapped(around_far, around_near), links, odd_inverse, False, odd_field, result,
    )
    image_at = lambda time, n: image[time, n]
    rest_at = lambda time, n: result[time, n] - about[...] * image[time, n]
    sums[...] = jnp.broadcast_to(
        in_lanes(row[...], {5: column_sum(rest_at, rest_at), 6: column_sum(rest_at, image_at)}),
        sums.shape,
    )


def final_kernel(sums, own, *outs):
    core, chip = lax.rem(lax.axis_index("sub"), 2), lax.axis_index("sub") // 2
    table = sums[...]
    first_lane = lax.broadcasted_iota(jnp.int32, table.shape, 1) == 0
    norm, crossed, about, rest, rest_first, image_rest, image_cross, image_norm = [
        table if n == 0 else pltpu.roll(table, 128 - n, 1) for n in range(8)
    ]
    whole = lambda x: jnp.sum(
        jnp.sum(jnp.where(first_lane, x, 0.0), axis=0, keepdims=True), axis=1, keepdims=True
    )
    norm_all, crossed_all = whole(norm), whole(crossed)
    alpha = norm_all / crossed_all
    off = about - crossed_all / norm_all
    norm_next = alpha * alpha * whole(rest + 2.0 * off * rest_first + off * off * norm)
    beta = norm_next / norm_all
    off = about - (1.0 + beta) / alpha
    curved = alpha * alpha * whole(
        image_rest + 2.0 * off * image_cross + off * off * image_norm
    )
    alpha_next = norm_next / curved
    of_first = jnp.broadcast_to(alpha + alpha_next * (1.0 + beta), (8, 128))
    of_second = jnp.broadcast_to(-alpha * alpha_next, (8, 128))
    for time in range(2):
        for n in range(8):
            even = of_first * own[0, n, time] + of_second * own[1, n, time]
            odd = own[2, n, time] + KAPPA * (
                of_first * own[3, n, time] + of_second * own[4, n, time]
            )
            for place, value in ((n, even), (8 + n, odd)):
                quarters = [value[2 * q : 2 * q + 2] for q in range(4)]
                for low in range(2):
                    halves = [
                        lax.select(core != low, quarters[2 * q + 1], quarters[2 * q])
                        for q in range(2)
                    ]
                    for high in range(2):
                        outs[2 * high + low][place, time] = lax.select(
                            chip != high, halves[1], halves[0]
                        )


VMEM = pl.BlockSpec(memory_space=pltpu.VMEM)
SMEM = pl.BlockSpec(memory_space=pltpu.SMEM)
ANY = pl.BlockSpec(memory_space=pl.ANY)


def call(kernel, name, shapes, scalars, arrays, scratch=(), outside=()):
    return pl.pallas_call(
        kernel,
        out_shape=tuple(jax.ShapeDtypeStruct(s, F32) for s in shapes),
        in_specs=[SMEM] * len(scalars)
        + [ANY if n in outside else VMEM for n in range(len(arrays))],
        out_specs=tuple(VMEM for _ in shapes),
        scratch_shapes=[pltpu.VMEM(s, F32) for s in scratch],
        compiler_params=pltpu.CompilerParams(vmem_limit_bytes=16 * 1024 * 1024),
        name=name,
    )(*scalars, *arrays)


FIELD = (2, 24, 8, 128)
EDGE = (24, 8, 128)


def device_of(vector, place):
    length = lax.axis_size("lat")
    return (vector ^ (2 * (place // (length // 2)))) * length + place


def swap(far, near):
    length, vectors = lax.axis_size("lat"), range(lax.axis_size("sub"))

    def moved(array, partner):
        pairs = [
            (device_of(v, i), device_of(v, partner(i))) for v in vectors for i in range(length)
        ]
        return lax.ppermute(array, ("sub", "lat"), pairs)

    return (
        moved(far, lambda i: (i + (1 if i % 2 else -1)) % length),
        moved(near, lambda i: i ^ 1),
    )


def whole(noise, colours, probe_rows, links, even, odd_inverse):
    (own,) = call(
        pack_kernel,
        "pack",
        ((50,) + noise.shape[4:],),
        (),
        (noise.reshape((48,) + noise.shape[4:]), colours),
    )
    gathered = lax.all_gather(own, "sub")
    probes_odd, turned, *sent = call(
        start_kernel,
        "start",
        (FIELD, FIELD, (12, 8, 128), (12, 8, 128)),
        (probe_rows,),
        (gathered, links[1, 3], odd_inverse),
        ((25, 2, 8, 128),),
    )
    got = swap(*sent)
    probes_even, partial = call(
        own_rhs_kernel,
        "own_rhs",
        (FIELD, FIELD),
        (probe_rows,),
        (gathered, turned, links),
        ((25, 2, 8, 128),),
    )
    around = swap(
        *call(
            around_kernel,
            "around",
            ((36, 8, 128),) * 2,
            (),
            (links, odd_inverse, turned),
            (),
            (2,),
        )
    )
    vector, odd, *sent = call(
        rhs_kernel, "rhs", (FIELD, FIELD, EDGE, EDGE), (), (partial, *got, links, odd_inverse)
    )
    kept = []
    for step in range(3):
        got = swap(*sent)
        (direct,) = call(direct_kernel, "direct%d" % step, (FIELD,), (), (vector, even))
        arrays = (direct, odd, *sent, *got, *around, links, odd_inverse)
        keep = step == 1
        vector, odd, *sent = call(
            functools.partial(step_kernel, step % 2 == 0),
            "step%d" % step,
            (FIELD, FIELD, EDGE, EDGE) + (FIELD,) * keep,
            (),
            arrays,
            () if keep else (FIELD,),
        )
        if keep:
            first_odd = sent.pop()
        kept.append(vector)
    first, image, second = kept
    got = swap(*sent)
    (direct,) = call(direct_kernel, "direct3", (FIELD,), (), (second, even))
    row, about = call(
        sums_kernel, "sums", ((1, 128), (8, 128)), (), (first, image, second)
    )
    second_odd, sums = call(
        last_kernel,
        "last",
        (FIELD, (lax.axis_size("lat"), 128)),
        (),
        (direct, odd, *sent, *got, *around, links, odd_inverse, image, row, about),
        (FIELD,),
    )
    (own_traces,) = call(
        traces_kernel,
        "traces",
        ((5, 8, 2, 8, 128),),
        (),
        (probes_even, probes_odd, turned, first, first_odd, second, second_odd),
    )
    groups = [
        [device_of(v, i) for i in range(lax.axis_size("lat"))] for v in range(lax.axis_size("sub"))
    ]
    sums = lax.all_to_all(
        sums, ("sub", "lat"), 0, 0, tiled=True, axis_index_groups=groups
    )
    traces = call(
        final_kernel, "final", ((16, 2, 2, 128),) * 4, (), (sums, own_traces)
    )
    total = traces[0]
    for n in (3, 2, 1):
        total = total + lax.ppermute(traces[n], "sub", [(i, i ^ n) for i in range(4)])
    return total.reshape(2, 2, 4, 2, 2, 128)


def solution(mesh):
    placed = (
        P(None, None, None, None, "lat", "sub", None),
        P(None, "lat", "sub", None),
        P(),
        P(None, None, None, None, None, "lat", None, None),
        P(None, None, None, None, "lat", None, None),
        P(None, None, None, None, "lat", None, None),
    )
    return jax.shard_map(
        whole,
        mesh=mesh,
        in_specs=placed,
        out_specs=P(None, None, None, "lat", "sub", None),
        check_vma=False,
    )
```

```python
import functools

import jax
import jax.numpy as jnp
from jax import lax
from jax.experimental import pallas as pl
from jax.experimental.pallas import tpu as pltpu
from jax.sharding import PartitionSpec as P

KAPPA = 0.135
F32 = jnp.float32

TURN = (
    ((1, 1), (0, 1)),
    ((1, 0), (0, 2)),
    ((0, 1), (1, 3)),
    ((0, 0), (1, 0)),
)
PAIRS = tuple((i, j) for i in range(6) for j in range(i + 1, 6))


def plus(x, y, power):
    power = power % 4
    if power == 0:
        return (x[0] + y[0], x[1] + y[1])
    if power == 1:
        return (x[0] - y[1], x[1] + y[0])
    if power == 2:
        return (x[0] - y[0], x[1] - y[1])
    return (x[0] + y[1], x[1] - y[0])


def mul(x, y):
    return (x[0] * y[0] - x[1] * y[1], x[0] * y[1] + x[1] * y[0])


def mul_conj(x, y):
    return (x[0] * y[0] + x[1] * y[1], x[0] * y[1] - x[1] * y[0])


def project(spinor, hop_dir, sign):
    if hop_dir == 3:
        extra = 0 if sign > 0 else 2
    else:
        extra = 2 if sign > 0 else 0
    return [
        [
            plus(spinor[s][a], spinor[2 + TURN[hop_dir][s][0]][a], TURN[hop_dir][s][1] + extra)
            for a in range(3)
        ]
        for s in range(2)
    ]


def expand_onto(total, half, hop_dir, sign):
    extra = 0 if sign > 0 else 2
    for s in range(2):
        source, power = TURN[hop_dir][s]
        for a in range(3):
            total[s][a] = half[s][a] if total[s][a] is None else plus(total[s][a], half[s][a], 0)
            if total[2 + s][a] is None:
                zero = jnp.zeros_like(half[source][a][0])
                total[2 + s][a] = plus((zero, zero), half[source][a], power + extra)
            else:
                total[2 + s][a] = plus(total[2 + s][a], half[source][a], power + extra)
    return total


def link_at(links, parity, hop_dir, time):
    return [
        [
            (
                links[parity, hop_dir, 0, i, j, time].astype(F32),
                links[parity, hop_dir, 1, i, j, time].astype(F32),
            )
            for j in range(3)
        ]
        for i in range(3)
    ]


def link_mul(link, half):
    out = []
    for s in range(2):
        row = []
        for i in range(3):
            total = mul(link[i][0], half[s][0])
            for j in (1, 2):
                total = plus(total, mul(link[i][j], half[s][j]), 0)
            row.append(total)
        out.append(row)
    return out


def link_mul_adj(link, half):
    out = []
    for s in range(2):
        row = []
        for i in range(3):
            total = mul_conj(link[0][i], half[s][0])
            for j in (1, 2):
                total = plus(total, mul_conj(link[j][i], half[s][j]), 0)
            row.append(total)
        out.append(row)
    return out


def shift_x(half, time, parity, offset):
    shape = (8, 128)
    depth = lax.broadcasted_iota(jnp.int32, shape, 0)
    lane = lax.broadcasted_iota(jnp.int32, shape, 1)
    row = (depth + lane // 4 + (time + parity)) % 2
    wanted = 1 if offset > 0 else 0
    moved = (lane // 4) * 4 + (lane + offset) % 4
    index = jnp.where(row == wanted, moved, lane)
    pick = lambda v: jnp.take_along_axis(v, index, axis=1, mode="promise_in_bounds")
    return [[(pick(v[0]), pick(v[1])) for v in r] for r in half]


def shift(half, hop_dir, time, parity, offset):
    if hop_dir == 0:
        return shift_x(half, time, parity, offset)
    if hop_dir == 1:
        pick = lambda v: pltpu.roll(v, (-4 * offset) % 128, 1)
    else:
        pick = lambda v: pltpu.roll(v, (-offset) % 8, 0)
    return [[(pick(v[0]), pick(v[1])) for v in r] for r in half]


def load_spinor(ref, *lead):
    return [
        [(ref[(*lead, s * 3 + a)], ref[(*lead, 12 + s * 3 + a)]) for a in range(3)]
        for s in range(4)
    ]


def store_spinor(ref, spinor, *lead):
    for s in range(4):
        for a in range(3):
            ref[(*lead, s * 3 + a)] = spinor[s][a][0]
            ref[(*lead, 12 + s * 3 + a)] = spinor[s][a][1]


class Swapped:

    def __init__(self, far, near):
        self.far, self.near = far, near
        self.odd = lax.rem(lax.axis_index("lat"), 2) == 1

    def high(self, n):
        return lax.select(self.odd, self.far[n], self.near[n])

    def low(self, n):
        return lax.select(self.odd, self.near[n], self.far[n])

    def put(self, n, for_earlier, for_later):
        self.far[n] = lax.select(self.odd, for_later, for_earlier)
        self.near[n] = lax.select(self.odd, for_earlier, for_later)


def load_half(row, base=0):
    return [
        [(row(base + s * 3 + a), row(base + 6 + s * 3 + a)) for a in range(3)] for s in range(2)
    ]


def store_halves(edges, for_earlier, for_later, base):
    at_first, at_last = edge_signs()
    for s in range(2):
        for a in range(3):
            for part in range(2):
                edges.put(
                    base + part * 6 + s * 3 + a,
                    for_earlier[s][a][part] * at_first,
                    for_later[s][a][part] * at_last,
                )


def scaled_half(half, factor):
    return [[(v[0] * factor, v[1] * factor) for v in r] for r in half]


def add_half(x, y):
    return [[plus(x[s][a], y[s][a], 0) for a in range(3)] for s in range(2)]


def hop_at(field, links, time, parity, dagger, high=None, low=None):
    forward, backward = (1, -1) if dagger else (-1, 1)
    total = [[None] * 3 for _ in range(4)]
    own = load_spinor(field, time)
    for hop_dir in range(3):
        half = shift(project(own, hop_dir, forward), hop_dir, time, parity, 1)
        half = link_mul(link_at(links, parity, hop_dir, time), half)
        expand_onto(total, half, hop_dir, forward)
        half = link_mul_adj(
            link_at(links, 1 - parity, hop_dir, time), project(own, hop_dir, backward)
        )
        expand_onto(total, shift(half, hop_dir, time, parity, -1), hop_dir, backward)
    if time == 0:
        half = project(load_spinor(field, 1), 3, forward)
        expand_onto(total, link_mul(link_at(links, parity, 3, 0), half), 3, forward)
        if low is not None:
            expand_onto(total, low, 3, backward)
    else:
        half = project(load_spinor(field, 0), 3, backward)
        expand_onto(total, link_mul_adj(link_at(links, 1 - parity, 3, 0), half), 3, backward)
        if high is not None:
            expand_onto(total, link_mul(link_at(links, parity, 3, 1), high), 3, forward)
    return total


def block_at(clover, chiral, time):
    diagonal = [clover[chiral, 0, i, i, time].astype(F32) for i in range(6)]
    upper = {
        (i, j): (
            clover[chiral, 0, i, j, time].astype(F32),
            clover[chiral, 1, i, j, time].astype(F32),
        )
        for i, j in PAIRS
    }
    return diagonal, upper


def block_packed(row):
    diagonal = [row(i) for i in range(6)]
    upper = {pair: (row(6 + 2 * n), row(7 + 2 * n)) for n, pair in enumerate(PAIRS)}
    return diagonal, upper


def block_mul(block, half):
    diagonal, upper = block
    flat = half[0] + half[1]
    out = [(diagonal[i] * flat[i][0], diagonal[i] * flat[i][1]) for i in range(6)]
    for i, j in PAIRS:
        out[i] = plus(out[i], mul(upper[i, j], flat[j]), 0)
        out[j] = plus(out[j], mul_conj(upper[i, j], flat[i]), 0)
    return [out[:3], out[3:]]


def clover_at(clover, spinor, time):
    return block_mul(block_at(clover, 0, time), spinor[:2]) + block_mul(
        block_at(clover, 1, time), spinor[2:]
    )


def edge_signs():
    position = lax.axis_index("lat")
    last = lax.axis_size("lat") - 1
    at_first = jnp.where(position == 0, -1.0, 1.0).astype(F32)
    at_last = jnp.where(position == last, -1.0, 1.0).astype(F32)
    return at_first, at_last


def begin_schur(vector, links, odd_inverse, dagger, partial, sent):
    forward, backward = (1, -1) if dagger else (-1, 1)
    for time in range(2):
        store_spinor(
            partial, clover_at(odd_inverse, hop_at(vector, links, time, 1, dagger), time), time
        )
    for base, field, parity in ((0, vector, 0), (12, partial, 1)):
        earlier = project(load_spinor(field, 0), 3, forward)
        later = project(load_spinor(field, 1), 3, backward)
        store_halves(sent, earlier, link_mul_adj(link_at(links, parity, 3, 1), later), base)


def end_schur(
    direct, partial, sent, got, around, links, odd_inverse, dagger, odd_field, result
):
    forward, backward = (1, -1) if dagger else (-1, 1)
    at_first, at_last = edge_signs()
    for time in range(2):
        if time == 0:
            half, sign = load_half(got.low), backward
        else:
            half = link_mul(link_at(links, 1, 3, 1), load_half(got.high))
            sign = forward
        own = load_spinor(partial, time)
        top = block_mul(block_at(odd_inverse, 0, time), half)
        bottom = block_mul(block_at(odd_inverse, 1, time), half)
        whole = [[plus(own[s][a], top[s][a], 0) for a in range(3)] for s in range(2)] + [
            [plus(own[2 + s][a], bottom[s][a], 0 if sign > 0 else 2) for a in range(3)]
            for s in range(2)
        ]
        store_spinor(odd_field, whole, time)
    back = block_mul(block_packed(around.high), load_half(sent.high))
    high = add_half(load_half(got.high, 12), scaled_half(back, at_last))
    back = block_mul(block_packed(around.low), load_half(sent.low))
    low = add_half(load_half(got.low, 12), scaled_half(back, at_first))
    for time in range(2):
        returned = hop_at(odd_field, links, time, 0, dagger, high, low)
        own = load_spinor(direct, time)
        factor = KAPPA * KAPPA
        store_spinor(
            result,
            [
                [
                    (
                        own[s][a][0] - factor * returned[s][a][0],
                        own[s][a][1] - factor * returned[s][a][1],
                    )
                    for a in range(3)
                ]
                for s in range(4)
            ],
            time,
        )


def around_kernel(links, odd_inverse, _, far, near):
    blocks = []
    for time in range(2):
        diagonal0, upper0 = block_at(odd_inverse, 0, time)
        diagonal1, upper1 = block_at(odd_inverse, 1, time)
        blocks.append(
            (
                [x - y for x, y in zip(diagonal0, diagonal1)],
                {pair: plus(upper0[pair], upper1[pair], 2) for pair in PAIRS},
            )
        )
    diagonal, upper = blocks[0]
    earlier = diagonal + [part for pair in PAIRS for part in upper[pair]]
    later = [None] * 36
    diagonal, upper = blocks[1]

    def entry(i, j):
        if i == j:
            return (diagonal[i], jnp.zeros_like(diagonal[i]))
        if i < j:
            return upper[i, j]
        value = upper[j, i]
        return (value[0], -value[1])

    link = link_at(links, 1, 3, 1)
    for s0, s1 in ((0, 0), (0, 1), (1, 1)):
        right = [[None] * 3 for _ in range(3)]
        for a in range(3):
            for b in range(3):
                total = mul(entry(s0 * 3 + a, s1 * 3), link[0][b])
                for c in (1, 2):
                    total = plus(total, mul(entry(s0 * 3 + a, s1 * 3 + c), link[c][b]), 0)
                right[a][b] = total
        for a in range(3):
            for b in range(3):
                if s0 == s1 and a > b:
                    continue
                total = mul_conj(link[0][a], right[0][b])
                for c in (1, 2):
                    total = plus(total, mul_conj(link[c][a], right[c][b]), 0)
                i, j = s0 * 3 + a, s1 * 3 + b
                if i == j:
                    later[i] = total[0]
                else:
                    n = PAIRS.index((i, j))
                    later[6 + 2 * n], later[7 + 2 * n] = total
    edges = Swapped(far, near)
    for n in range(36):
        edges.put(n, earlier[n], later[n])


def pack_kernel(noise, colours, out):
    out[:48] = noise[...]
    out[48:] = colours[...].astype(F32)


def vector_index():
    upper = lax.axis_index("lat") // (lax.axis_size("lat") // 2)
    return jnp.bitwise_xor(lax.axis_index("sub"), 2 * upper)


def unpack_probes(probe_rows, gathered, raw, parity, probes):
    probe_row = probe_rows[vector_index()]
    for q in range(4):
        raw[:24, :, 2 * q : 2 * q + 2, :] = gathered[q, 24 * parity : 24 * parity + 24]
        raw[24, :, 2 * q : 2 * q + 2, :] = gathered[q, 48 + parity]
    for time in range(2):
        masked = jnp.bitwise_and(raw[24, time].astype(jnp.int32), probe_row)
        masked = jnp.bitwise_xor(masked, jnp.right_shift(masked, 2))
        masked = jnp.bitwise_xor(masked, jnp.right_shift(masked, 1))
        sign = (1 - 2 * jnp.bitwise_and(masked, 1)).astype(F32)
        for n in range(24):
            probes[time, n] = raw[n, time] * sign


def start_kernel(probe_rows, gathered, time_link, odd_inverse, probes, turned, far, near, raw):
    unpack_probes(probe_rows, gathered, raw, 1, probes)
    for time in range(2):
        store_spinor(turned, clover_at(odd_inverse, load_spinor(probes, time), time), time)
    link = [
        [(time_link[0, i, j, 1].astype(F32), time_link[1, i, j, 1].astype(F32)) for j in range(3)]
        for i in range(3)
    ]
    half = link_mul_adj(link, project(load_spinor(turned, 1), 3, 1))
    store_halves(Swapped(far, near), project(load_spinor(turned, 0), 3, -1), half, 0)


def own_rhs_kernel(probe_rows, gathered, turned, links, probes, rhs, raw):
    unpack_probes(probe_rows, gathered, raw, 0, probes)
    for time in range(2):
        total = hop_at(turned, links, time, 0, False)
        own = load_spinor(probes, time)
        store_spinor(
            rhs,
            [
                [
                    (own[s][a][0] + KAPPA * total[s][a][0], own[s][a][1] + KAPPA * total[s][a][1])
                    for a in range(3)
                ]
                for s in range(4)
            ],
            time,
        )


def direct_kernel(vector, even, out):
    for time in range(2):
        store_spinor(out, clover_at(even, load_spinor(vector, time), time), time)


def rhs_kernel(partial, got_far, got_near, links, odd_inverse, rhs, odd, far, near):
    got = Swapped(got_far, got_near)
    half = scaled_half(load_half(got.low), KAPPA)
    store_spinor(rhs, expand_onto(load_spinor(partial, 0), half, 3, 1), 0)
    half = scaled_half(link_mul(link_at(links, 0, 3, 1), load_half(got.high)), KAPPA)
    store_spinor(rhs, expand_onto(load_spinor(partial, 1), half, 3, -1), 1)
    begin_schur(rhs, links, odd_inverse, True, odd, Swapped(far, near))


def step_kernel(
    dagger,
    direct, partial, sent_far, sent_near, got_far, got_near, around_far, around_near,
    links, odd_inverse,
    result, odd, far, near, odd_field,
):
    end_schur(
        direct, partial, Swapped(sent_far, sent_near), Swapped(got_far, got_near),
        Swapped(around_far, around_near), links, odd_inverse, dagger, odd_field, result,
    )
    begin_schur(result, links, odd_inverse, not dagger, odd, Swapped(far, near))


def column_sum(left, right):
    total = None
    for time in range(2):
        for n in range(24):
            term = left(time, n) * right(time, n)
            total = term if total is None else total + term
    return jnp.sum(total, axis=0, keepdims=True)


def traces_at(left, right):
    def dot(s, r):
        total = mul_conj(left[s][0], right[r][0])
        for a in (1, 2):
            total = plus(total, mul_conj(left[s][a], right[r][a]), 0)
        return total

    up = [[dot(s, 2 + r) for r in range(2)] for s in range(2)]
    down = [[dot(2 + s, r) for r in range(2)] for s in range(2)]
    x_sum = plus(plus(down[0][1], down[1][0], 0), plus(up[0][1], up[1][0], 0), 2)
    y_sum = plus(plus(down[0][1], down[1][0], 2), plus(up[0][1], up[1][0], 2), 2)
    z_sum = plus(plus(down[0][0], down[1][1], 2), plus(up[0][0], up[1][1], 2), 2)
    t_sum = plus(plus(down[0][0], down[1][1], 0), plus(up[0][0], up[1][1], 0), 0)
    columns = ((-x_sum[1], x_sum[0]), y_sum, (-z_sum[1], z_sum[0]), t_sum)
    return [columns[hop_dir][part] for part in range(2) for hop_dir in range(4)]


def store_traces(outs, base, probes, field, time):
    core, chip = lax.rem(lax.axis_index("sub"), 2), lax.axis_index("sub") // 2
    for n, value in enumerate(traces_at(load_spinor(probes, time), load_spinor(field, time))):
        quarters = [value[2 * q : 2 * q + 2] for q in range(4)]
        for low in range(2):
            halves = [
                lax.select(core != low, quarters[2 * q + 1], quarters[2 * q]) for q in range(2)
            ]
            for high in range(2):
                outs[2 * high + low][base + n, time] = lax.select(
                    chip != high, halves[1], halves[0]
                )


def traces_kernel(probes_even, probes_odd, turned, first, first_odd, second, *outs):
    for time in range(2):
        store_traces(outs, 0, probes_even, first, time)
        store_traces(outs, 8, probes_even, second, time)
        store_traces(outs, 16, probes_odd, first_odd, time)
        store_traces(outs, 24, probes_odd, turned, time)


def last_traces_kernel(probes_odd, second_odd, *outs):
    for time in range(2):
        store_traces(outs, 0, probes_odd, second_odd, time)


def in_lanes(row, values):
    lane = lax.broadcasted_iota(jnp.int32, (1, 128), 1)
    for n, value in values.items():
        value = jnp.broadcast_to(jnp.sum(value, axis=1, keepdims=True), (1, 128))
        row = jnp.where(lane == n, value, row)
    return row


def sums_kernel(first, image, vector, row, about):
    first_at = lambda time, n: first[time, n]
    image_at = lambda time, n: image[time, n]
    vector_at = lambda time, n: vector[time, n]
    whole = lambda x: jnp.sum(x, axis=1, keepdims=True)
    norm = column_sum(first_at, first_at)
    image_norm = column_sum(image_at, image_at)
    norm_all = whole(norm)
    shift_by = jnp.broadcast_to(
        whole(image_norm) / jnp.where(norm_all > 0, norm_all, 1.0), (8, 128)
    )
    about[...] = shift_by
    rest_at = lambda time, n: vector[time, n] - shift_by * first[time, n]
    lane = lax.broadcasted_iota(jnp.int32, (1, 128), 1)
    row[...] = in_lanes(
        jnp.where(lane == 2, shift_by[:1], 0.0),
        {
            0: norm,
            1: column_sum(first_at, vector_at),
            3: column_sum(rest_at, rest_at),
            4: column_sum(rest_at, first_at),
            7: image_norm,
        },
    )


def last_kernel(
    direct, partial, sent_far, sent_near, got_far, got_near, around_far, around_near,
    links, odd_inverse, image, row, about,
    odd_field, sums, result,
):
    end_schur(
        direct, partial, Swapped(sent_far, sent_near), Swapped(got_far, got_near),
        Swapped(around_far, around_near), links, odd_inverse, False, odd_field, result,
    )
    image_at = lambda time, n: image[time, n]
    rest_at = lambda time, n: result[time, n] - about[...] * image[time, n]
    sums[...] = jnp.broadcast_to(
        in_lanes(row[...], {5: column_sum(rest_at, rest_at), 6: column_sum(rest_at, image_at)}),
        sums.shape,
    )


def factors(table):
    first_lane = lax.broadcasted_iota(jnp.int32, table.shape, 1) == 0
    norm, crossed, about, rest, rest_first, image_rest, image_cross, image_norm = [
        table if n == 0 else pltpu.roll(table, 128 - n, 1) for n in range(8)
    ]
    whole = lambda x: jnp.sum(
        jnp.sum(jnp.where(first_lane, x, 0.0), axis=0, keepdims=True), axis=1, keepdims=True
    )
    norm_all, crossed_all = whole(norm), whole(crossed)
    alpha = norm_all / crossed_all
    off = about - crossed_all / norm_all
    norm_next = alpha * alpha * whole(rest + 2.0 * off * rest_first + off * off * norm)
    beta = norm_next / norm_all
    off = about - (1.0 + beta) / alpha
    curved = alpha * alpha * whole(
        image_rest + 2.0 * off * image_cross + off * off * image_norm
    )
    alpha_next = norm_next / curved
    return [
        jnp.broadcast_to(value, (2, 128))
        for value in (alpha + alpha_next * (1.0 + beta), -alpha * alpha_next)
    ]


def final_kernel(sums, *refs):
    early, late, out = refs[:4], refs[4:8], refs[8]
    length = lax.axis_size("lat")
    half = length // 2
    by_vector = []
    for vector in range(4):
        lower = sums[vector * length : vector * length + half]
        upper = sums[(vector ^ 2) * length + half : (vector ^ 2) * length + length]
        by_vector.append(factors(jnp.concatenate([lower, upper], axis=0)))
    mine = vector_index()
    core, chip = lax.rem(mine, 2), mine // 2
    weights = []
    for peer in range(4):
        weights.append([])
        for n in range(2):
            halves = [
                lax.select(
                    core != peer % 2, by_vector[2 * q + 1][n], by_vector[2 * q][n]
                )
                for q in range(2)
            ]
            weights[-1].append(lax.select(chip != peer // 2, halves[1], halves[0]))
    for time in range(2):
        for n in range(8):
            even = odd = plain = None
            for peer, (of_first, of_second) in enumerate(weights):
                ref, last = early[peer], late[peer]
                even_part = of_first * ref[n, time] + of_second * ref[8 + n, time]
                odd_part = of_first * ref[16 + n, time] + of_second * last[n, time]
                plain_part = ref[24 + n, time]
                even = even_part if even is None else even + even_part
                odd = odd_part if odd is None else odd + odd_part
                plain = plain_part if plain is None else plain + plain_part
            out[n, time] = even
            out[8 + n, time] = plain + KAPPA * odd


VMEM = pl.BlockSpec(memory_space=pltpu.VMEM)
SMEM = pl.BlockSpec(memory_space=pltpu.SMEM)
ANY = pl.BlockSpec(memory_space=pl.ANY)


def call(kernel, name, shapes, scalars, arrays, scratch=(), outside=()):
    return pl.pallas_call(
        kernel,
        out_shape=tuple(jax.ShapeDtypeStruct(s, F32) for s in shapes),
        in_specs=[SMEM] * len(scalars)
        + [ANY if n in outside else VMEM for n in range(len(arrays))],
        out_specs=tuple(VMEM for _ in shapes),
        scratch_shapes=[pltpu.VMEM(s, F32) for s in scratch],
        compiler_params=pltpu.CompilerParams(vmem_limit_bytes=16 * 1024 * 1024),
        name=name,
    )(*scalars, *arrays)


FIELD = (2, 24, 8, 128)
EDGE = (24, 8, 128)


def device_of(vector, place):
    length = lax.axis_size("lat")
    return (vector ^ (2 * (place // (length // 2)))) * length + place


def swap(far, near):
    length, vectors = lax.axis_size("lat"), range(lax.axis_size("sub"))

    def moved(array, partner):
        pairs = [
            (device_of(v, i), device_of(v, partner(i))) for v in vectors for i in range(length)
        ]
        return lax.ppermute(array, ("sub", "lat"), pairs)

    return (
        moved(far, lambda i: (i + (1 if i % 2 else -1)) % length),
        moved(near, lambda i: i ^ 1),
    )


def swap_depths(traces):
    subs = range(lax.axis_size("sub"))
    return [traces[0]] + [
        lax.ppermute(traces[n], "sub", [(i, i ^ n) for i in subs]) for n in (1, 2, 3)
    ]


def whole(noise, colours, probe_rows, links, even, odd_inverse):
    (own,) = call(
        pack_kernel,
        "pack",
        ((50,) + noise.shape[4:],),
        (),
        (noise.reshape((48,) + noise.shape[4:]), colours),
    )
    gathered = lax.all_gather(own, "sub")
    probes_odd, turned, *sent = call(
        start_kernel,
        "start",
        (FIELD, FIELD, (12, 8, 128), (12, 8, 128)),
        (probe_rows,),
        (gathered, links[1, 3], odd_inverse),
        ((25, 2, 8, 128),),
    )
    got = swap(*sent)
    probes_even, partial = call(
        own_rhs_kernel,
        "own_rhs",
        (FIELD, FIELD),
        (probe_rows,),
        (gathered, turned, links),
        ((25, 2, 8, 128),),
    )
    around = swap(
        *call(
            around_kernel,
            "around",
            ((36, 8, 128),) * 2,
            (),
            (links, odd_inverse, turned),
            (),
            (2,),
        )
    )
    vector, odd, *sent = call(
        rhs_kernel, "rhs", (FIELD, FIELD, EDGE, EDGE), (), (partial, *got, links, odd_inverse)
    )
    kept = []
    for step in range(3):
        got = swap(*sent)
        (direct,) = call(direct_kernel, "direct%d" % step, (FIELD,), (), (vector, even))
        arrays = (direct, odd, *sent, *got, *around, links, odd_inverse)
        keep = step == 1
        vector, odd, *sent = call(
            functools.partial(step_kernel, step % 2 == 0),
            "step%d" % step,
            (FIELD, FIELD, EDGE, EDGE) + (FIELD,) * keep,
            (),
            arrays,
            () if keep else (FIELD,),
        )
        if keep:
            first_odd = sent.pop()
        kept.append(vector)
    first, image, second = kept
    got = swap(*sent)
    (direct,) = call(direct_kernel, "direct3", (FIELD,), (), (second, even))
    row, about = call(
        sums_kernel, "sums", ((1, 128), (8, 128)), (), (first, image, second)
    )
    early = swap_depths(
        call(
            traces_kernel,
            "traces",
            ((32, 2, 2, 128),) * 4,
            (),
            (probes_even, probes_odd, turned, first, first_odd, second),
        )
    )
    devices = lax.axis_size("lat") * lax.axis_size("sub")
    second_odd, sums = call(
        last_kernel,
        "last",
        (FIELD, (devices, 128)),
        (),
        (direct, odd, *sent, *got, *around, links, odd_inverse, image, row, about),
        (FIELD,),
    )
    sums = lax.all_to_all(sums, ("sub", "lat"), 0, 0, tiled=True)
    late = swap_depths(
        call(last_traces_kernel, "last_traces", ((8, 2, 2, 128),) * 4, (), (probes_odd, second_odd))
    )
    (out,) = call(final_kernel, "final", ((16, 2, 2, 128),), (), (sums, *early, *late))
    return out.reshape(2, 2, 4, 2, 2, 128)


def solution(mesh):
    placed = (
        P(None, None, None, None, "lat", "sub", None),
        P(None, "lat", "sub", None),
        P(),
        P(None, None, None, None, None, "lat", None, None),
        P(None, None, None, None, "lat", None, None),
        P(None, None, None, None, "lat", None, None),
    )
    return jax.shard_map(
        whole,
        mesh=mesh,
        in_specs=placed,
        out_specs=P(None, None, None, "lat", "sub", None),
        check_vma=False,
    )
```

```python
import functools

import jax
import jax.numpy as jnp
from jax import lax
from jax.experimental import pallas as pl
from jax.experimental.pallas import tpu as pltpu
from jax.sharding import PartitionSpec as P

KAPPA = 0.135
F32 = jnp.float32

TURN = (
    ((1, 1), (0, 1)),
    ((1, 0), (0, 2)),
    ((0, 1), (1, 3)),
    ((0, 0), (1, 0)),
)
PAIRS = tuple((i, j) for i in range(6) for j in range(i + 1, 6))


def plus(x, y, power):
    power = power % 4
    if power == 0:
        return (x[0] + y[0], x[1] + y[1])
    if power == 1:
        return (x[0] - y[1], x[1] + y[0])
    if power == 2:
        return (x[0] - y[0], x[1] - y[1])
    return (x[0] + y[1], x[1] - y[0])


def mul(x, y):
    return (x[0] * y[0] - x[1] * y[1], x[0] * y[1] + x[1] * y[0])


def mul_conj(x, y):
    return (x[0] * y[0] + x[1] * y[1], x[0] * y[1] - x[1] * y[0])


def project(spinor, hop_dir, sign):
    if hop_dir == 3:
        extra = 0 if sign > 0 else 2
    else:
        extra = 2 if sign > 0 else 0
    return [
        [
            plus(spinor[s][a], spinor[2 + TURN[hop_dir][s][0]][a], TURN[hop_dir][s][1] + extra)
            for a in range(3)
        ]
        for s in range(2)
    ]


def expand_onto(total, half, hop_dir, sign):
    extra = 0 if sign > 0 else 2
    for s in range(2):
        source, power = TURN[hop_dir][s]
        for a in range(3):
            total[s][a] = half[s][a] if total[s][a] is None else plus(total[s][a], half[s][a], 0)
            if total[2 + s][a] is None:
                zero = jnp.zeros_like(half[source][a][0])
                total[2 + s][a] = plus((zero, zero), half[source][a], power + extra)
            else:
                total[2 + s][a] = plus(total[2 + s][a], half[source][a], power + extra)
    return total


def link_at(links, parity, hop_dir, time):
    return [
        [
            (
                links[parity, hop_dir, 0, i, j, time].astype(F32),
                links[parity, hop_dir, 1, i, j, time].astype(F32),
            )
            for j in range(3)
        ]
        for i in range(3)
    ]


def link_mul(link, half):
    out = []
    for s in range(2):
        row = []
        for i in range(3):
            total = mul(link[i][0], half[s][0])
            for j in (1, 2):
                total = plus(total, mul(link[i][j], half[s][j]), 0)
            row.append(total)
        out.append(row)
    return out


def link_mul_adj(link, half):
    out = []
    for s in range(2):
        row = []
        for i in range(3):
            total = mul_conj(link[0][i], half[s][0])
            for j in (1, 2):
                total = plus(total, mul_conj(link[j][i], half[s][j]), 0)
            row.append(total)
        out.append(row)
    return out


def shift_x(half, time, parity, offset):
    shape = (8, 128)
    depth = lax.broadcasted_iota(jnp.int32, shape, 0)
    lane = lax.broadcasted_iota(jnp.int32, shape, 1)
    row = (depth + lane // 4 + (time + parity)) % 2
    wanted = 1 if offset > 0 else 0
    moved = (lane // 4) * 4 + (lane + offset) % 4
    index = jnp.where(row == wanted, moved, lane)
    pick = lambda v: jnp.take_along_axis(v, index, axis=1, mode="promise_in_bounds")
    return [[(pick(v[0]), pick(v[1])) for v in r] for r in half]


def shift(half, hop_dir, time, parity, offset):
    if hop_dir == 0:
        return shift_x(half, time, parity, offset)
    if hop_dir == 1:
        pick = lambda v: pltpu.roll(v, (-4 * offset) % 128, 1)
    else:
        pick = lambda v: pltpu.roll(v, (-offset) % 8, 0)
    return [[(pick(v[0]), pick(v[1])) for v in r] for r in half]


def load_spinor(ref, *lead):
    return [
        [(ref[(*lead, s * 3 + a)], ref[(*lead, 12 + s * 3 + a)]) for a in range(3)]
        for s in range(4)
    ]


def store_spinor(ref, spinor, *lead):
    for s in range(4):
        for a in range(3):
            ref[(*lead, s * 3 + a)] = spinor[s][a][0]
            ref[(*lead, 12 + s * 3 + a)] = spinor[s][a][1]


class Swapped:

    def __init__(self, far, near):
        self.far, self.near = far, near
        self.odd = lax.rem(lax.axis_index("lat"), 2) == 1

    def high(self, n):
        return lax.select(self.odd, self.far[n], self.near[n])

    def low(self, n):
        return lax.select(self.odd, self.near[n], self.far[n])

    def put(self, n, for_earlier, for_later):
        self.far[n] = lax.select(self.odd, for_later, for_earlier)
        self.near[n] = lax.select(self.odd, for_earlier, for_later)


def load_half(row, base=0):
    return [
        [(row(base + s * 3 + a), row(base + 6 + s * 3 + a)) for a in range(3)] for s in range(2)
    ]


def store_halves(edges, for_earlier, for_later, base):
    at_first, at_last = edge_signs()
    for s in range(2):
        for a in range(3):
            for part in range(2):
                edges.put(
                    base + part * 6 + s * 3 + a,
                    for_earlier[s][a][part] * at_first,
                    for_later[s][a][part] * at_last,
                )


def scaled_half(half, factor):
    return [[(v[0] * factor, v[1] * factor) for v in r] for r in half]


def add_half(x, y):
    return [[plus(x[s][a], y[s][a], 0) for a in range(3)] for s in range(2)]


def hop_at(field, links, time, parity, dagger, high=None, low=None):
    forward, backward = (1, -1) if dagger else (-1, 1)
    total = [[None] * 3 for _ in range(4)]
    own = load_spinor(field, time)
    for hop_dir in range(3):
        half = shift(project(own, hop_dir, forward), hop_dir, time, parity, 1)
        half = link_mul(link_at(links, parity, hop_dir, time), half)
        expand_onto(total, half, hop_dir, forward)
        half = link_mul_adj(
            link_at(links, 1 - parity, hop_dir, time), project(own, hop_dir, backward)
        )
        expand_onto(total, shift(half, hop_dir, time, parity, -1), hop_dir, backward)
    if time == 0:
        half = project(load_spinor(field, 1), 3, forward)
        expand_onto(total, link_mul(link_at(links, parity, 3, 0), half), 3, forward)
        if low is not None:
            expand_onto(total, low, 3, backward)
    else:
        half = project(load_spinor(field, 0), 3, backward)
        expand_onto(total, link_mul_adj(link_at(links, 1 - parity, 3, 0), half), 3, backward)
        if high is not None:
            expand_onto(total, link_mul(link_at(links, parity, 3, 1), high), 3, forward)
    return total


def block_at(clover, chiral, time):
    diagonal = [clover[chiral, 0, i, i, time].astype(F32) for i in range(6)]
    upper = {
        (i, j): (
            clover[chiral, 0, i, j, time].astype(F32),
            clover[chiral, 1, i, j, time].astype(F32),
        )
        for i, j in PAIRS
    }
    return diagonal, upper


def block_packed(row):
    diagonal = [row(i) for i in range(6)]
    upper = {pair: (row(6 + 2 * n), row(7 + 2 * n)) for n, pair in enumerate(PAIRS)}
    return diagonal, upper


def block_mul(block, half):
    diagonal, upper = block
    flat = half[0] + half[1]
    out = [(diagonal[i] * flat[i][0], diagonal[i] * flat[i][1]) for i in range(6)]
    for i, j in PAIRS:
        out[i] = plus(out[i], mul(upper[i, j], flat[j]), 0)
        out[j] = plus(out[j], mul_conj(upper[i, j], flat[i]), 0)
    return [out[:3], out[3:]]


def clover_at(clover, spinor, time):
    return block_mul(block_at(clover, 0, time), spinor[:2]) + block_mul(
        block_at(clover, 1, time), spinor[2:]
    )


def edge_signs():
    position = lax.axis_index("lat")
    last = lax.axis_size("lat") - 1
    at_first = jnp.where(position == 0, -1.0, 1.0).astype(F32)
    at_last = jnp.where(position == last, -1.0, 1.0).astype(F32)
    return at_first, at_last


def begin_slice(vector, links, odd_inverse, dagger, time, partial, edge):
    side = (1 if dagger else -1) * (1 if time == 0 else -1)
    sign = edge_signs()[time]
    whole = clover_at(odd_inverse, hop_at(vector, links, time, 1, dagger), time)
    store_spinor(partial, whole)
    for base, spinor, parity in ((0, load_spinor(vector, time), 0), (12, whole, 1)):
        half = project(spinor, 3, side)
        if time == 1:
            half = link_mul_adj(link_at(links, parity, 3, 1), half)
        for s in range(2):
            for a in range(3):
                for part in range(2):
                    edge[base + part * 6 + s * 3 + a] = half[s][a][part] * sign


def begin_schur(vector, links, odd_inverse, dagger, far_side, partial, edge):
    odd = lax.rem(lax.axis_index("lat"), 2) == 1
    later = odd if far_side else jnp.logical_not(odd)

    @pl.when(later)
    def _():
        begin_slice(vector, links, odd_inverse, dagger, 1, partial, edge)

    @pl.when(jnp.logical_not(later))
    def _():
        begin_slice(vector, links, odd_inverse, dagger, 0, partial, edge)


def spinor_of(row):
    return [[(row(s * 3 + a), row(12 + s * 3 + a)) for a in range(3)] for s in range(4)]


def end_schur(direct, back, partial, got, links, odd_inverse, dagger, odd_field, result):
    forward, backward = (1, -1) if dagger else (-1, 1)
    for time in range(2):
        if time == 0:
            half, sign = load_half(got.low), backward
        else:
            half = link_mul(link_at(links, 1, 3, 1), load_half(got.high))
            sign = forward
        own = spinor_of(partial.low if time == 0 else partial.high)
        top = block_mul(block_at(odd_inverse, 0, time), half)
        bottom = block_mul(block_at(odd_inverse, 1, time), half)
        whole = [[plus(own[s][a], top[s][a], 0) for a in range(3)] for s in range(2)] + [
            [plus(own[2 + s][a], bottom[s][a], 0 if sign > 0 else 2) for a in range(3)]
            for s in range(2)
        ]
        store_spinor(odd_field, whole, time)
    kept = lambda n: back[n]
    high = add_half(load_half(got.high, 12), load_half(kept))
    low = add_half(load_half(got.low, 12), load_half(kept, 12))
    for time in range(2):
        returned = hop_at(odd_field, links, time, 0, dagger, high, low)
        own = load_spinor(direct, time)
        factor = KAPPA * KAPPA
        store_spinor(
            result,
            [
                [
                    (
                        own[s][a][0] - factor * returned[s][a][0],
                        own[s][a][1] - factor * returned[s][a][1],
                    )
                    for a in range(3)
                ]
                for s in range(4)
            ],
            time,
        )


def around_kernel(links, odd_inverse, _, far, near):
    blocks = []
    for time in range(2):
        diagonal0, upper0 = block_at(odd_inverse, 0, time)
        diagonal1, upper1 = block_at(odd_inverse, 1, time)
        blocks.append(
            (
                [x - y for x, y in zip(diagonal0, diagonal1)],
                {pair: plus(upper0[pair], upper1[pair], 2) for pair in PAIRS},
            )
        )
    diagonal, upper = blocks[0]
    earlier = diagonal + [part for pair in PAIRS for part in upper[pair]]
    later = [None] * 36
    diagonal, upper = blocks[1]

    def entry(i, j):
        if i == j:
            return (diagonal[i], jnp.zeros_like(diagonal[i]))
        if i < j:
            return upper[i, j]
        value = upper[j, i]
        return (value[0], -value[1])

    link = link_at(links, 1, 3, 1)
    for s0, s1 in ((0, 0), (0, 1), (1, 1)):
        right = [[None] * 3 for _ in range(3)]
        for a in range(3):
            for b in range(3):
                total = mul(entry(s0 * 3 + a, s1 * 3), link[0][b])
                for c in (1, 2):
                    total = plus(total, mul(entry(s0 * 3 + a, s1 * 3 + c), link[c][b]), 0)
                right[a][b] = total
        for a in range(3):
            for b in range(3):
                if s0 == s1 and a > b:
                    continue
                total = mul_conj(link[0][a], right[0][b])
                for c in (1, 2):
                    total = plus(total, mul_conj(link[c][a], right[c][b]), 0)
                i, j = s0 * 3 + a, s1 * 3 + b
                if i == j:
                    later[i] = total[0]
                else:
                    n = PAIRS.index((i, j))
                    later[6 + 2 * n], later[7 + 2 * n] = total
    edges = Swapped(far, near)
    for n in range(36):
        edges.put(n, earlier[n], later[n])


def pack_kernel(noise, colours, out):
    out[:48] = noise[...]
    out[48:] = colours[...].astype(F32)


def vector_index():
    upper = lax.axis_index("lat") // (lax.axis_size("lat") // 2)
    return jnp.bitwise_xor(lax.axis_index("sub"), 2 * upper)


def unpack_probes(probe_rows, gathered, raw, parity, probes):
    probe_row = probe_rows[vector_index()]
    for q in range(4):
        raw[:24, :, 2 * q : 2 * q + 2, :] = gathered[q, 24 * parity : 24 * parity + 24]
        raw[24, :, 2 * q : 2 * q + 2, :] = gathered[q, 48 + parity]
    for time in range(2):
        masked = jnp.bitwise_and(raw[24, time].astype(jnp.int32), probe_row)
        masked = jnp.bitwise_xor(masked, jnp.right_shift(masked, 2))
        masked = jnp.bitwise_xor(masked, jnp.right_shift(masked, 1))
        sign = (1 - 2 * jnp.bitwise_and(masked, 1)).astype(F32)
        for n in range(24):
            probes[time, n] = raw[n, time] * sign


def start_kernel(probe_rows, gathered, time_link, odd_inverse, probes, turned, far, near, raw):
    unpack_probes(probe_rows, gathered, raw, 1, probes)
    for time in range(2):
        store_spinor(turned, clover_at(odd_inverse, load_spinor(probes, time), time), time)
    link = [
        [(time_link[0, i, j, 1].astype(F32), time_link[1, i, j, 1].astype(F32)) for j in range(3)]
        for i in range(3)
    ]
    half = link_mul_adj(link, project(load_spinor(turned, 1), 3, 1))
    store_halves(Swapped(far, near), project(load_spinor(turned, 0), 3, -1), half, 0)


def own_rhs_kernel(probe_rows, gathered, turned, links, probes, rhs, raw):
    unpack_probes(probe_rows, gathered, raw, 0, probes)
    for time in range(2):
        total = hop_at(turned, links, time, 0, False)
        own = load_spinor(probes, time)
        store_spinor(
            rhs,
            [
                [
                    (own[s][a][0] + KAPPA * total[s][a][0], own[s][a][1] + KAPPA * total[s][a][1])
                    for a in range(3)
                ]
                for s in range(4)
            ],
            time,
        )


def direct_kernel(
    vector, even, sent_far, sent_near, around_far, around_near, out, back
):
    for time in range(2):
        store_spinor(out, clover_at(even, load_spinor(vector, time), time), time)
    sent, around = Swapped(sent_far, sent_near), Swapped(around_far, around_near)
    at_first, at_last = edge_signs()
    for base, matrix, half, sign in (
        (0, around.high, sent.high, at_last),
        (12, around.low, sent.low, at_first),
    ):
        half = block_mul(block_packed(matrix), load_half(half))
        for s in range(2):
            for a in range(3):
                for part in range(2):
                    back[base + part * 6 + s * 3 + a] = half[s][a][part] * sign


def rhs_kernel(partial, got_far, got_near, links, odd_inverse, rhs, odd, far):
    got = Swapped(got_far, got_near)
    half = scaled_half(load_half(got.low), KAPPA)
    store_spinor(rhs, expand_onto(load_spinor(partial, 0), half, 3, 1), 0)
    half = scaled_half(link_mul(link_at(links, 0, 3, 1), load_half(got.high)), KAPPA)
    store_spinor(rhs, expand_onto(load_spinor(partial, 1), half, 3, -1), 1)
    begin_schur(rhs, links, odd_inverse, True, True, odd, far)


def near_kernel(dagger, vector, links, odd_inverse, odd, near):
    begin_schur(vector, links, odd_inverse, dagger, False, odd, near)


def step_kernel(
    dagger,
    direct, back, odd_far, odd_near, got_far, got_near, links, odd_inverse,
    result, odd, far, odd_field,
):
    end_schur(
        direct, back, Swapped(odd_far, odd_near), Swapped(got_far, got_near),
        links, odd_inverse, dagger, odd_field, result,
    )
    begin_schur(result, links, odd_inverse, not dagger, True, odd, far)


def column_sum(left, right):
    total = None
    for time in range(2):
        for n in range(24):
            term = left(time, n) * right(time, n)
            total = term if total is None else total + term
    return jnp.sum(total, axis=0, keepdims=True)


def traces_at(left, right):
    def dot(s, r):
        total = mul_conj(left[s][0], right[r][0])
        for a in (1, 2):
            total = plus(total, mul_conj(left[s][a], right[r][a]), 0)
        return total

    up = [[dot(s, 2 + r) for r in range(2)] for s in range(2)]
    down = [[dot(2 + s, r) for r in range(2)] for s in range(2)]
    x_sum = plus(plus(down[0][1], down[1][0], 0), plus(up[0][1], up[1][0], 0), 2)
    y_sum = plus(plus(down[0][1], down[1][0], 2), plus(up[0][1], up[1][0], 2), 2)
    z_sum = plus(plus(down[0][0], down[1][1], 2), plus(up[0][0], up[1][1], 2), 2)
    t_sum = plus(plus(down[0][0], down[1][1], 0), plus(up[0][0], up[1][1], 0), 0)
    columns = ((-x_sum[1], x_sum[0]), y_sum, (-z_sum[1], z_sum[0]), t_sum)
    return [columns[hop_dir][part] for part in range(2) for hop_dir in range(4)]


def store_traces(outs, base, probes, field, time):
    core, chip = lax.rem(lax.axis_index("sub"), 2), lax.axis_index("sub") // 2
    for n, value in enumerate(traces_at(load_spinor(probes, time), load_spinor(field, time))):
        quarters = [value[2 * q : 2 * q + 2] for q in range(4)]
        for low in range(2):
            halves = [
                lax.select(core != low, quarters[2 * q + 1], quarters[2 * q]) for q in range(2)
            ]
            for high in range(2):
                outs[2 * high + low][base + n, time] = lax.select(
                    chip != high, halves[1], halves[0]
                )


def traces_kernel(probes_even, probes_odd, turned, first, first_odd, second, *outs):
    for time in range(2):
        store_traces(outs, 0, probes_even, first, time)
        store_traces(outs, 8, probes_even, second, time)
        store_traces(outs, 16, probes_odd, first_odd, time)
        store_traces(outs, 24, probes_odd, turned, time)


def last_traces_kernel(probes_odd, second_odd, *outs):
    for time in range(2):
        store_traces(outs, 0, probes_odd, second_odd, time)


def in_lanes(row, values):
    lane = lax.broadcasted_iota(jnp.int32, (1, 128), 1)
    for n, value in values.items():
        value = jnp.broadcast_to(jnp.sum(value, axis=1, keepdims=True), (1, 128))
        row = jnp.where(lane == n, value, row)
    return row


def sums_kernel(first, image, vector, row, about):
    first_at = lambda time, n: first[time, n]
    image_at = lambda time, n: image[time, n]
    vector_at = lambda time, n: vector[time, n]
    whole = lambda x: jnp.sum(x, axis=1, keepdims=True)
    norm = column_sum(first_at, first_at)
    image_norm = column_sum(image_at, image_at)
    norm_all = whole(norm)
    shift_by = jnp.broadcast_to(
        whole(image_norm) / jnp.where(norm_all > 0, norm_all, 1.0), (8, 128)
    )
    about[...] = shift_by
    rest_at = lambda time, n: vector[time, n] - shift_by * first[time, n]
    lane = lax.broadcasted_iota(jnp.int32, (1, 128), 1)
    row[...] = in_lanes(
        jnp.where(lane == 2, shift_by[:1], 0.0),
        {
            0: norm,
            1: column_sum(first_at, vector_at),
            3: column_sum(rest_at, rest_at),
            4: column_sum(rest_at, first_at),
            7: image_norm,
        },
    )


def last_kernel(
    direct, back, odd_far, odd_near, got_far, got_near, links, odd_inverse, image, row, about,
    odd_field, sums, result,
):
    end_schur(
        direct, back, Swapped(odd_far, odd_near), Swapped(got_far, got_near),
        links, odd_inverse, False, odd_field, result,
    )
    image_at = lambda time, n: image[time, n]
    rest_at = lambda time, n: result[time, n] - about[...] * image[time, n]
    sums[...] = jnp.broadcast_to(
        in_lanes(row[...], {5: column_sum(rest_at, rest_at), 6: column_sum(rest_at, image_at)}),
        sums.shape,
    )


def factors(table):
    first_lane = lax.broadcasted_iota(jnp.int32, table.shape, 1) == 0
    norm, crossed, about, rest, rest_first, image_rest, image_cross, image_norm = [
        table if n == 0 else pltpu.roll(table, 128 - n, 1) for n in range(8)
    ]
    whole = lambda x: jnp.sum(
        jnp.sum(jnp.where(first_lane, x, 0.0), axis=0, keepdims=True), axis=1, keepdims=True
    )
    norm_all, crossed_all = whole(norm), whole(crossed)
    alpha = norm_all / crossed_all
    off = about - crossed_all / norm_all
    norm_next = alpha * alpha * whole(rest + 2.0 * off * rest_first + off * off * norm)
    beta = norm_next / norm_all
    off = about - (1.0 + beta) / alpha
    curved = alpha * alpha * whole(
        image_rest + 2.0 * off * image_cross + off * off * image_norm
    )
    alpha_next = norm_next / curved
    return [
        jnp.broadcast_to(value, (2, 128))
        for value in (alpha + alpha_next * (1.0 + beta), -alpha * alpha_next)
    ]


def final_kernel(sums, *refs):
    early, late, out = refs[:4], refs[4:8], refs[8]
    length = lax.axis_size("lat")
    half = length // 2
    by_vector = []
    for vector in range(4):
        lower = sums[vector * length : vector * length + half]
        upper = sums[(vector ^ 2) * length + half : (vector ^ 2) * length + length]
        by_vector.append(factors(jnp.concatenate([lower, upper], axis=0)))
    mine = vector_index()
    core, chip = lax.rem(mine, 2), mine // 2
    weights = []
    for peer in range(4):
        weights.append([])
        for n in range(2):
            halves = [
                lax.select(
                    core != peer % 2, by_vector[2 * q + 1][n], by_vector[2 * q][n]
                )
                for q in range(2)
            ]
            weights[-1].append(lax.select(chip != peer // 2, halves[1], halves[0]))
    for time in range(2):
        for n in range(8):
            even = odd = plain = None
            for peer, (of_first, of_second) in enumerate(weights):
                ref, last = early[peer], late[peer]
                even_part = of_first * ref[n, time] + of_second * ref[8 + n, time]
                odd_part = of_first * ref[16 + n, time] + of_second * last[n, time]
                plain_part = ref[24 + n, time]
                even = even_part if even is None else even + even_part
                odd = odd_part if odd is None else odd + odd_part
                plain = plain_part if plain is None else plain + plain_part
            out[n, time] = even
            out[8 + n, time] = plain + KAPPA * odd


VMEM = pl.BlockSpec(memory_space=pltpu.VMEM)
SMEM = pl.BlockSpec(memory_space=pltpu.SMEM)
ANY = pl.BlockSpec(memory_space=pl.ANY)


def call(kernel, name, shapes, scalars, arrays, scratch=(), outside=()):
    return pl.pallas_call(
        kernel,
        out_shape=tuple(jax.ShapeDtypeStruct(s, F32) for s in shapes),
        in_specs=[SMEM] * len(scalars)
        + [ANY if n in outside else VMEM for n in range(len(arrays))],
        out_specs=tuple(VMEM for _ in shapes),
        scratch_shapes=[pltpu.VMEM(s, F32) for s in scratch],
        compiler_params=pltpu.CompilerParams(vmem_limit_bytes=16 * 1024 * 1024),
        name=name,
    )(*scalars, *arrays)


FIELD = (2, 24, 8, 128)
EDGE = (24, 8, 128)


def device_of(vector, place):
    length = lax.axis_size("lat")
    return (vector ^ (2 * (place // (length // 2)))) * length + place


def swap(array, far_side):
    length, vectors = lax.axis_size("lat"), range(lax.axis_size("sub"))
    partner = (lambda i: (i + (1 if i % 2 else -1)) % length) if far_side else (lambda i: i ^ 1)
    pairs = [(device_of(v, i), device_of(v, partner(i))) for v in vectors for i in range(length)]
    return lax.ppermute(array, ("sub", "lat"), pairs)


def swap_depths(traces):
    subs = range(lax.axis_size("sub"))
    return [traces[0]] + [
        lax.ppermute(traces[n], "sub", [(i, i ^ n) for i in subs]) for n in (1, 2, 3)
    ]


def whole(noise, colours, probe_rows, links, even, odd_inverse):
    (own,) = call(
        pack_kernel,
        "pack",
        ((50,) + noise.shape[4:],),
        (),
        (noise.reshape((48,) + noise.shape[4:]), colours),
    )
    gathered = lax.all_gather(own, "sub")
    probes_odd, turned, *sent = call(
        start_kernel,
        "start",
        (FIELD, FIELD, (12, 8, 128), (12, 8, 128)),
        (probe_rows,),
        (gathered, links[1, 3], odd_inverse),
        ((25, 2, 8, 128),),
    )
    got = (swap(sent[0], True), swap(sent[1], False))
    probes_even, partial = call(
        own_rhs_kernel,
        "own_rhs",
        (FIELD, FIELD),
        (probe_rows,),
        (gathered, turned, links),
        ((25, 2, 8, 128),),
    )
    around = call(
        around_kernel,
        "around",
        ((36, 8, 128),) * 2,
        (),
        (links, odd_inverse, turned),
        (),
        (2,),
    )
    around = (swap(around[0], True), swap(around[1], False))

    def exchange(vector, odd, far, dagger, name):
        got_far = swap(far, True)
        odd_near, near = call(
            functools.partial(near_kernel, dagger),
            "near" + name,
            (EDGE, EDGE),
            (),
            (vector, links, odd_inverse),
        )
        got_near = swap(near, False)
        direct, back = call(
            direct_kernel, "direct" + name, (FIELD, EDGE), (), (vector, even, far, near, *around)
        )
        return (direct, back, odd, odd_near, got_far, got_near, links, odd_inverse)

    vector, odd, far = call(
        rhs_kernel, "rhs", (FIELD, EDGE, EDGE), (), (partial, *got, links, odd_inverse)
    )
    kept = []
    for step in range(3):
        dagger = step % 2 == 0
        arrays = exchange(vector, odd, far, dagger, str(step))
        keep = step == 1
        vector, odd, far, *rest = call(
            functools.partial(step_kernel, dagger),
            "step%d" % step,
            (FIELD, EDGE, EDGE) + (FIELD,) * keep,
            (),
            arrays,
            () if keep else (FIELD,),
        )
        if keep:
            first_odd = rest[0]
        kept.append(vector)
    first, image, second = kept
    arrays = exchange(second, odd, far, False, "3")
    row, about = call(
        sums_kernel, "sums", ((1, 128), (8, 128)), (), (first, image, second)
    )
    early = swap_depths(
        call(
            traces_kernel,
            "traces",
            ((32, 2, 2, 128),) * 4,
            (),
            (probes_even, probes_odd, turned, first, first_odd, second),
        )
    )
    devices = lax.axis_size("lat") * lax.axis_size("sub")
    second_odd, sums = call(
        last_kernel,
        "last",
        (FIELD, (devices, 128)),
        (),
        (*arrays, image, row, about),
        (FIELD,),
    )
    sums = lax.all_to_all(sums, ("sub", "lat"), 0, 0, tiled=True)
    late = swap_depths(
        call(last_traces_kernel, "last_traces", ((8, 2, 2, 128),) * 4, (), (probes_odd, second_odd))
    )
    (out,) = call(final_kernel, "final", ((16, 2, 2, 128),), (), (sums, *early, *late))
    return out.reshape(2, 2, 4, 2, 2, 128)


def solution(mesh):
    placed = (
        P(None, None, None, None, "lat", "sub", None),
        P(None, "lat", "sub", None),
        P(),
        P(None, None, None, None, None, "lat", None, None),
        P(None, None, None, None, "lat", None, None),
        P(None, None, None, None, "lat", None, None),
    )
    return jax.shard_map(
        whole,
        mesh=mesh,
        in_specs=placed,
        out_specs=P(None, None, None, "lat", "sub", None),
        check_vma=False,
    )
```

```python
import functools

import jax
import jax.numpy as jnp
from jax import lax
from jax.experimental import pallas as pl
from jax.experimental.pallas import tpu as pltpu
from jax.sharding import PartitionSpec as P

KAPPA = 0.135
F32 = jnp.float32

TURN = (
    ((1, 1), (0, 1)),
    ((1, 0), (0, 2)),
    ((0, 1), (1, 3)),
    ((0, 0), (1, 0)),
)
PAIRS = tuple((i, j) for i in range(6) for j in range(i + 1, 6))


def plus(x, y, power):
    power = power % 4
    if power == 0:
        return (x[0] + y[0], x[1] + y[1])
    if power == 1:
        return (x[0] - y[1], x[1] + y[0])
    if power == 2:
        return (x[0] - y[0], x[1] - y[1])
    return (x[0] + y[1], x[1] - y[0])


def mul(x, y):
    return (x[0] * y[0] - x[1] * y[1], x[0] * y[1] + x[1] * y[0])


def mul_conj(x, y):
    return (x[0] * y[0] + x[1] * y[1], x[0] * y[1] - x[1] * y[0])


def project(spinor, hop_dir, sign):
    if hop_dir == 3:
        extra = 0 if sign > 0 else 2
    else:
        extra = 2 if sign > 0 else 0
    return [
        [
            plus(spinor[s][a], spinor[2 + TURN[hop_dir][s][0]][a], TURN[hop_dir][s][1] + extra)
            for a in range(3)
        ]
        for s in range(2)
    ]


def expand_onto(total, half, hop_dir, sign):
    extra = 0 if sign > 0 else 2
    for s in range(2):
        source, power = TURN[hop_dir][s]
        for a in range(3):
            total[s][a] = half[s][a] if total[s][a] is None else plus(total[s][a], half[s][a], 0)
            if total[2 + s][a] is None:
                zero = jnp.zeros_like(half[source][a][0])
                total[2 + s][a] = plus((zero, zero), half[source][a], power + extra)
            else:
                total[2 + s][a] = plus(total[2 + s][a], half[source][a], power + extra)
    return total


def link_at(links, parity, hop_dir, time):
    return [
        [
            (
                links[parity, hop_dir, 0, i, j, time].astype(F32),
                links[parity, hop_dir, 1, i, j, time].astype(F32),
            )
            for j in range(3)
        ]
        for i in range(3)
    ]


def link_mul(link, half):
    out = []
    for s in range(2):
        row = []
        for i in range(3):
            total = mul(link[i][0], half[s][0])
            for j in (1, 2):
                total = plus(total, mul(link[i][j], half[s][j]), 0)
            row.append(total)
        out.append(row)
    return out


def link_mul_adj(link, half):
    out = []
    for s in range(2):
        row = []
        for i in range(3):
            total = mul_conj(link[0][i], half[s][0])
            for j in (1, 2):
                total = plus(total, mul_conj(link[j][i], half[s][j]), 0)
            row.append(total)
        out.append(row)
    return out


def shift_x(half, time, parity, offset):
    shape = (8, 128)
    depth = lax.broadcasted_iota(jnp.int32, shape, 0)
    lane = lax.broadcasted_iota(jnp.int32, shape, 1)
    row = (depth + lane // 4 + (time + parity)) % 2
    wanted = 1 if offset > 0 else 0
    moved = (lane // 4) * 4 + (lane + offset) % 4
    index = jnp.where(row == wanted, moved, lane)
    pick = lambda v: jnp.take_along_axis(v, index, axis=1, mode="promise_in_bounds")
    return [[(pick(v[0]), pick(v[1])) for v in r] for r in half]


def shift(half, hop_dir, time, parity, offset):
    if hop_dir == 0:
        return shift_x(half, time, parity, offset)
    if hop_dir == 1:
        pick = lambda v: pltpu.roll(v, (-4 * offset) % 128, 1)
    else:
        pick = lambda v: pltpu.roll(v, (-offset) % 8, 0)
    return [[(pick(v[0]), pick(v[1])) for v in r] for r in half]


def load_spinor(ref, *lead):
    return [
        [(ref[(*lead, s * 3 + a)], ref[(*lead, 12 + s * 3 + a)]) for a in range(3)]
        for s in range(4)
    ]


def store_spinor(ref, spinor, *lead):
    for s in range(4):
        for a in range(3):
            ref[(*lead, s * 3 + a)] = spinor[s][a][0]
            ref[(*lead, 12 + s * 3 + a)] = spinor[s][a][1]


class Swapped:

    def __init__(self, far, near):
        self.far, self.near = far, near
        self.odd = lax.rem(lax.axis_index("lat"), 2) == 1

    def high(self, n):
        return lax.select(self.odd, self.far[n], self.near[n])

    def low(self, n):
        return lax.select(self.odd, self.near[n], self.far[n])

    def put(self, n, for_earlier, for_later):
        self.far[n] = lax.select(self.odd, for_later, for_earlier)
        self.near[n] = lax.select(self.odd, for_earlier, for_later)


def load_half(row, base=0):
    return [
        [(row(base + s * 3 + a), row(base + 6 + s * 3 + a)) for a in range(3)] for s in range(2)
    ]


def store_halves(edges, for_earlier, for_later, base):
    at_first, at_last = edge_signs()
    for s in range(2):
        for a in range(3):
            for part in range(2):
                edges.put(
                    base + part * 6 + s * 3 + a,
                    for_earlier[s][a][part] * at_first,
                    for_later[s][a][part] * at_last,
                )


def scaled_half(half, factor):
    return [[(v[0] * factor, v[1] * factor) for v in r] for r in half]


def add_half(x, y):
    return [[plus(x[s][a], y[s][a], 0) for a in range(3)] for s in range(2)]


def hop_at(field, links, time, parity, dagger, high=None, low=None):
    forward, backward = (1, -1) if dagger else (-1, 1)
    total = [[None] * 3 for _ in range(4)]
    own = load_spinor(field, time)
    for hop_dir in range(3):
        half = shift(project(own, hop_dir, forward), hop_dir, time, parity, 1)
        half = link_mul(link_at(links, parity, hop_dir, time), half)
        expand_onto(total, half, hop_dir, forward)
        half = link_mul_adj(
            link_at(links, 1 - parity, hop_dir, time), project(own, hop_dir, backward)
        )
        expand_onto(total, shift(half, hop_dir, time, parity, -1), hop_dir, backward)
    if time == 0:
        half = project(load_spinor(field, 1), 3, forward)
        expand_onto(total, link_mul(link_at(links, parity, 3, 0), half), 3, forward)
        if low is not None:
            expand_onto(total, low, 3, backward)
    else:
        half = project(load_spinor(field, 0), 3, backward)
        expand_onto(total, link_mul_adj(link_at(links, 1 - parity, 3, 0), half), 3, backward)
        if high is not None:
            expand_onto(total, link_mul(link_at(links, parity, 3, 1), high), 3, forward)
    return total


def block_at(clover, chiral, time):
    diagonal = [clover[chiral, 0, i, i, time].astype(F32) for i in range(6)]
    upper = {
        (i, j): (
            clover[chiral, 0, i, j, time].astype(F32),
            clover[chiral, 1, i, j, time].astype(F32),
        )
        for i, j in PAIRS
    }
    return diagonal, upper


def block_packed(row):
    diagonal = [row(i) for i in range(6)]
    upper = {pair: (row(6 + 2 * n), row(7 + 2 * n)) for n, pair in enumerate(PAIRS)}
    return diagonal, upper


def block_mul(block, half):
    diagonal, upper = block
    flat = half[0] + half[1]
    out = [(diagonal[i] * flat[i][0], diagonal[i] * flat[i][1]) for i in range(6)]
    for i, j in PAIRS:
        out[i] = plus(out[i], mul(upper[i, j], flat[j]), 0)
        out[j] = plus(out[j], mul_conj(upper[i, j], flat[i]), 0)
    return [out[:3], out[3:]]


def clover_at(clover, spinor, time):
    return block_mul(block_at(clover, 0, time), spinor[:2]) + block_mul(
        block_at(clover, 1, time), spinor[2:]
    )


def edge_signs():
    position = lax.axis_index("lat")
    last = lax.axis_size("lat") - 1
    at_first = jnp.where(position == 0, -1.0, 1.0).astype(F32)
    at_last = jnp.where(position == last, -1.0, 1.0).astype(F32)
    return at_first, at_last


def begin_slice(vector, links, odd_inverse, dagger, time, partial, edge):
    side = (1 if dagger else -1) * (1 if time == 0 else -1)
    sign = edge_signs()[time]
    whole = clover_at(odd_inverse, hop_at(vector, links, time, 1, dagger), time)
    store_spinor(partial, whole)
    for base, spinor, parity in ((0, load_spinor(vector, time), 0), (12, whole, 1)):
        half = project(spinor, 3, side)
        if time == 1:
            half = link_mul_adj(link_at(links, parity, 3, 1), half)
        for s in range(2):
            for a in range(3):
                for part in range(2):
                    edge[base + part * 6 + s * 3 + a] = half[s][a][part] * sign


def begin_schur(vector, links, odd_inverse, dagger, far_side, partial, edge):
    odd = lax.rem(lax.axis_index("lat"), 2) == 1
    later = odd if far_side else jnp.logical_not(odd)

    @pl.when(later)
    def _():
        begin_slice(vector, links, odd_inverse, dagger, 1, partial, edge)

    @pl.when(jnp.logical_not(later))
    def _():
        begin_slice(vector, links, odd_inverse, dagger, 0, partial, edge)


def spinor_of(row):
    return [[(row(s * 3 + a), row(12 + s * 3 + a)) for a in range(3)] for s in range(4)]


def end_schur(direct, back, partial, got, links, odd_inverse, dagger, odd_field, result):
    forward, backward = (1, -1) if dagger else (-1, 1)
    for time in range(2):
        if time == 0:
            half, sign = load_half(got.low), backward
        else:
            half = link_mul(link_at(links, 1, 3, 1), load_half(got.high))
            sign = forward
        own = spinor_of(partial.low if time == 0 else partial.high)
        top = block_mul(block_at(odd_inverse, 0, time), half)
        bottom = block_mul(block_at(odd_inverse, 1, time), half)
        whole = [[plus(own[s][a], top[s][a], 0) for a in range(3)] for s in range(2)] + [
            [plus(own[2 + s][a], bottom[s][a], 0 if sign > 0 else 2) for a in range(3)]
            for s in range(2)
        ]
        store_spinor(odd_field, whole, time)
    kept = lambda n: back[n]
    high = add_half(load_half(got.high, 12), load_half(kept))
    low = add_half(load_half(got.low, 12), load_half(kept, 12))
    for time in range(2):
        returned = hop_at(odd_field, links, time, 0, dagger, high, low)
        own = load_spinor(direct, time)
        factor = KAPPA * KAPPA
        store_spinor(
            result,
            [
                [
                    (
                        own[s][a][0] - factor * returned[s][a][0],
                        own[s][a][1] - factor * returned[s][a][1],
                    )
                    for a in range(3)
                ]
                for s in range(4)
            ],
            time,
        )


def around_kernel(links, odd_inverse, _, far, near):
    blocks = []
    for time in range(2):
        diagonal0, upper0 = block_at(odd_inverse, 0, time)
        diagonal1, upper1 = block_at(odd_inverse, 1, time)
        blocks.append(
            (
                [x - y for x, y in zip(diagonal0, diagonal1)],
                {pair: plus(upper0[pair], upper1[pair], 2) for pair in PAIRS},
            )
        )
    diagonal, upper = blocks[0]
    earlier = diagonal + [part for pair in PAIRS for part in upper[pair]]
    later = [None] * 36
    diagonal, upper = blocks[1]

    def entry(i, j):
        if i == j:
            return (diagonal[i], jnp.zeros_like(diagonal[i]))
        if i < j:
            return upper[i, j]
        value = upper[j, i]
        return (value[0], -value[1])

    link = link_at(links, 1, 3, 1)
    for s0, s1 in ((0, 0), (0, 1), (1, 1)):
        right = [[None] * 3 for _ in range(3)]
        for a in range(3):
            for b in range(3):
                total = mul(entry(s0 * 3 + a, s1 * 3), link[0][b])
                for c in (1, 2):
                    total = plus(total, mul(entry(s0 * 3 + a, s1 * 3 + c), link[c][b]), 0)
                right[a][b] = total
        for a in range(3):
            for b in range(3):
                if s0 == s1 and a > b:
                    continue
                total = mul_conj(link[0][a], right[0][b])
                for c in (1, 2):
                    total = plus(total, mul_conj(link[c][a], right[c][b]), 0)
                i, j = s0 * 3 + a, s1 * 3 + b
                if i == j:
                    later[i] = total[0]
                else:
                    n = PAIRS.index((i, j))
                    later[6 + 2 * n], later[7 + 2 * n] = total
    edges = Swapped(far, near)
    for n in range(36):
        edges.put(n, earlier[n], later[n])


def pack_kernel(noise, colours, out):
    out[:48] = noise[...]
    out[48:] = colours[...].astype(F32)


def vector_index():
    upper = lax.axis_index("lat") // (lax.axis_size("lat") // 2)
    return jnp.bitwise_xor(lax.axis_index("sub"), 2 * upper)


def unpack_probes(probe_rows, gathered, raw, parity, probes):
    probe_row = probe_rows[vector_index()]
    for q in range(4):
        raw[:24, :, 2 * q : 2 * q + 2, :] = gathered[q, 24 * parity : 24 * parity + 24]
        raw[24, :, 2 * q : 2 * q + 2, :] = gathered[q, 48 + parity]
    for time in range(2):
        masked = jnp.bitwise_and(raw[24, time].astype(jnp.int32), probe_row)
        masked = jnp.bitwise_xor(masked, jnp.right_shift(masked, 2))
        masked = jnp.bitwise_xor(masked, jnp.right_shift(masked, 1))
        sign = (1 - 2 * jnp.bitwise_and(masked, 1)).astype(F32)
        for n in range(24):
            probes[time, n] = raw[n, time] * sign


def start_kernel(probe_rows, gathered, time_link, odd_inverse, probes, turned, far, near, raw):
    unpack_probes(probe_rows, gathered, raw, 1, probes)
    for time in range(2):
        store_spinor(turned, clover_at(odd_inverse, load_spinor(probes, time), time), time)
    link = [
        [(time_link[0, i, j, 1].astype(F32), time_link[1, i, j, 1].astype(F32)) for j in range(3)]
        for i in range(3)
    ]
    half = link_mul_adj(link, project(load_spinor(turned, 1), 3, 1))
    store_halves(Swapped(far, near), project(load_spinor(turned, 0), 3, -1), half, 0)


def own_rhs_kernel(probe_rows, gathered, turned, links, probes, rhs, raw):
    unpack_probes(probe_rows, gathered, raw, 0, probes)
    for time in range(2):
        total = hop_at(turned, links, time, 0, False)
        own = load_spinor(probes, time)
        store_spinor(
            rhs,
            [
                [
                    (own[s][a][0] + KAPPA * total[s][a][0], own[s][a][1] + KAPPA * total[s][a][1])
                    for a in range(3)
                ]
                for s in range(4)
            ],
            time,
        )


def direct_kernel(
    vector, even, sent_far, sent_near, around_far, around_near, out, back
):
    for time in range(2):
        store_spinor(out, clover_at(even, load_spinor(vector, time), time), time)
    sent, around = Swapped(sent_far, sent_near), Swapped(around_far, around_near)
    at_first, at_last = edge_signs()
    for base, matrix, half, sign in (
        (0, around.high, sent.high, at_last),
        (12, around.low, sent.low, at_first),
    ):
        half = block_mul(block_packed(matrix), load_half(half))
        for s in range(2):
            for a in range(3):
                for part in range(2):
                    back[base + part * 6 + s * 3 + a] = half[s][a][part] * sign


def rhs_kernel(partial, got_far, got_near, links, odd_inverse, rhs, odd, far):
    got = Swapped(got_far, got_near)
    half = scaled_half(load_half(got.low), KAPPA)
    store_spinor(rhs, expand_onto(load_spinor(partial, 0), half, 3, 1), 0)
    half = scaled_half(link_mul(link_at(links, 0, 3, 1), load_half(got.high)), KAPPA)
    store_spinor(rhs, expand_onto(load_spinor(partial, 1), half, 3, -1), 1)
    begin_schur(rhs, links, odd_inverse, True, True, odd, far)


def near_kernel(dagger, vector, links, odd_inverse, odd, near):
    begin_schur(vector, links, odd_inverse, dagger, False, odd, near)


def step_kernel(
    dagger,
    direct, back, odd_far, odd_near, got_far, got_near, links, odd_inverse,
    result, odd, far, odd_field,
):
    end_schur(
        direct, back, Swapped(odd_far, odd_near), Swapped(got_far, got_near),
        links, odd_inverse, dagger, odd_field, result,
    )
    begin_schur(result, links, odd_inverse, not dagger, True, odd, far)


def column_sum(left, right):
    total = None
    for time in range(2):
        for n in range(24):
            term = left(time, n) * right(time, n)
            total = term if total is None else total + term
    return jnp.sum(total, axis=0, keepdims=True)


def traces_at(left, right):
    def dot(s, r):
        total = mul_conj(left[s][0], right[r][0])
        for a in (1, 2):
            total = plus(total, mul_conj(left[s][a], right[r][a]), 0)
        return total

    up = [[dot(s, 2 + r) for r in range(2)] for s in range(2)]
    down = [[dot(2 + s, r) for r in range(2)] for s in range(2)]
    x_sum = plus(plus(down[0][1], down[1][0], 0), plus(up[0][1], up[1][0], 0), 2)
    y_sum = plus(plus(down[0][1], down[1][0], 2), plus(up[0][1], up[1][0], 2), 2)
    z_sum = plus(plus(down[0][0], down[1][1], 2), plus(up[0][0], up[1][1], 2), 2)
    t_sum = plus(plus(down[0][0], down[1][1], 0), plus(up[0][0], up[1][1], 0), 0)
    columns = ((-x_sum[1], x_sum[0]), y_sum, (-z_sum[1], z_sum[0]), t_sum)
    return [columns[hop_dir][part] for part in range(2) for hop_dir in range(4)]


def store_traces(outs, base, probes, field, time):
    core, chip = lax.rem(lax.axis_index("sub"), 2), lax.axis_index("sub") // 2
    for n, value in enumerate(traces_at(load_spinor(probes, time), load_spinor(field, time))):
        quarters = [value[2 * q : 2 * q + 2] for q in range(4)]
        for low in range(2):
            halves = [
                lax.select(core != low, quarters[2 * q + 1], quarters[2 * q]) for q in range(2)
            ]
            for high in range(2):
                outs[2 * high + low][base + n, time] = lax.select(
                    chip != high, halves[1], halves[0]
                )


def traces_kernel(probes_even, probes_odd, turned, first, first_odd, second, *outs):
    for time in range(2):
        store_traces(outs, 0, probes_even, first, time)
        store_traces(outs, 8, probes_even, second, time)
        store_traces(outs, 16, probes_odd, first_odd, time)
        store_traces(outs, 24, probes_odd, turned, time)


def last_traces_kernel(probes_odd, second_odd, *outs):
    for time in range(2):
        store_traces(outs, 0, probes_odd, second_odd, time)


def in_lanes(row, values):
    lane = lax.broadcasted_iota(jnp.int32, (1, 128), 1)
    for n, value in values.items():
        value = jnp.broadcast_to(jnp.sum(value, axis=1, keepdims=True), (1, 128))
        row = jnp.where(lane == n, value, row)
    return row


def sums_kernel(first, image, vector, row, about):
    first_at = lambda time, n: first[time, n]
    image_at = lambda time, n: image[time, n]
    vector_at = lambda time, n: vector[time, n]
    whole = lambda x: jnp.sum(x, axis=1, keepdims=True)
    norm = column_sum(first_at, first_at)
    image_norm = column_sum(image_at, image_at)
    norm_all = whole(norm)
    shift_by = jnp.broadcast_to(
        whole(image_norm) / jnp.where(norm_all > 0, norm_all, 1.0), (8, 128)
    )
    about[...] = shift_by
    rest_at = lambda time, n: vector[time, n] - shift_by * first[time, n]
    lane = lax.broadcasted_iota(jnp.int32, (1, 128), 1)
    row[...] = in_lanes(
        jnp.where(lane == 2, shift_by[:1], 0.0),
        {
            0: norm,
            1: column_sum(first_at, vector_at),
            3: column_sum(rest_at, rest_at),
            4: column_sum(rest_at, first_at),
            7: image_norm,
        },
    )


def last_kernel(
    direct, back, odd_far, odd_near, got_far, got_near, links, odd_inverse, image, row, about,
    odd_field, sums, result,
):
    end_schur(
        direct, back, Swapped(odd_far, odd_near), Swapped(got_far, got_near),
        links, odd_inverse, False, odd_field, result,
    )
    image_at = lambda time, n: image[time, n]
    rest_at = lambda time, n: result[time, n] - about[...] * image[time, n]
    sums[...] = jnp.broadcast_to(
        in_lanes(row[...], {5: column_sum(rest_at, rest_at), 6: column_sum(rest_at, image_at)}),
        sums.shape,
    )


def factors(table):
    lane = lax.broadcasted_iota(jnp.int32, table.shape, 1)
    of_lane = lax.broadcasted_iota(jnp.int32, (1, 128), 1)
    total = lambda x: jnp.sum(x, axis=1, keepdims=True)
    columns = jnp.sum(table, axis=0, keepdims=True)
    norm_all = total(jnp.where(of_lane == 0, columns, 0.0))
    crossed_all = total(jnp.where(of_lane == 1, columns, 0.0))
    about = jnp.broadcast_to(table[:, 2:3], table.shape)

    def around_shift(shift_by, square, cross, norm):
        off = about - shift_by
        weight = jnp.where(lane == square, 1.0, 0.0)
        weight = jnp.where(lane == cross, 2.0 * off, weight)
        weight = jnp.where(lane == norm, off * off, weight)
        return total(jnp.sum(weight * table, axis=0, keepdims=True))

    alpha = norm_all / crossed_all
    norm_next = alpha * alpha * around_shift(crossed_all / norm_all, 3, 4, 0)
    beta = norm_next / norm_all
    curved = alpha * alpha * around_shift((1.0 + beta) / alpha, 5, 6, 7)
    alpha_next = norm_next / curved
    return [
        jnp.broadcast_to(value, (2, 128))
        for value in (alpha + alpha_next * (1.0 + beta), -alpha * alpha_next)
    ]


def final_kernel(sums, *refs):
    early, late, out = refs[:4], refs[4:8], refs[8]
    length = lax.axis_size("lat")
    half = length // 2
    by_vector = []
    for vector in range(4):
        lower = sums[vector * length : vector * length + half]
        upper = sums[(vector ^ 2) * length + half : (vector ^ 2) * length + length]
        by_vector.append(factors(jnp.concatenate([lower, upper], axis=0)))
    mine = vector_index()
    core, chip = lax.rem(mine, 2), mine // 2
    weights = []
    for peer in range(4):
        weights.append([])
        for n in range(2):
            halves = [
                lax.select(
                    core != peer % 2, by_vector[2 * q + 1][n], by_vector[2 * q][n]
                )
                for q in range(2)
            ]
            weights[-1].append(lax.select(chip != peer // 2, halves[1], halves[0]))
    for time in range(2):
        for n in range(8):
            even = odd = plain = None
            for peer, (of_first, of_second) in enumerate(weights):
                ref, last = early[peer], late[peer]
                even_part = of_first * ref[n, time] + of_second * ref[8 + n, time]
                odd_part = of_first * ref[16 + n, time] + of_second * last[n, time]
                plain_part = ref[24 + n, time]
                even = even_part if even is None else even + even_part
                odd = odd_part if odd is None else odd + odd_part
                plain = plain_part if plain is None else plain + plain_part
            out[n, time] = even
            out[8 + n, time] = plain + KAPPA * odd


VMEM = pl.BlockSpec(memory_space=pltpu.VMEM)
SMEM = pl.BlockSpec(memory_space=pltpu.SMEM)
ANY = pl.BlockSpec(memory_space=pl.ANY)


def call(kernel, name, shapes, scalars, arrays, scratch=(), outside=()):
    return pl.pallas_call(
        kernel,
        out_shape=tuple(jax.ShapeDtypeStruct(s, F32) for s in shapes),
        in_specs=[SMEM] * len(scalars)
        + [ANY if n in outside else VMEM for n in range(len(arrays))],
        out_specs=tuple(VMEM for _ in shapes),
        scratch_shapes=[pltpu.VMEM(s, F32) for s in scratch],
        compiler_params=pltpu.CompilerParams(vmem_limit_bytes=16 * 1024 * 1024),
        name=name,
    )(*scalars, *arrays)


FIELD = (2, 24, 8, 128)
EDGE = (24, 8, 128)


def device_of(vector, place):
    length = lax.axis_size("lat")
    return (vector ^ (2 * (place // (length // 2)))) * length + place


def swap(array, far_side):
    length, vectors = lax.axis_size("lat"), range(lax.axis_size("sub"))
    partner = (lambda i: (i + (1 if i % 2 else -1)) % length) if far_side else (lambda i: i ^ 1)
    pairs = [(device_of(v, i), device_of(v, partner(i))) for v in vectors for i in range(length)]
    return lax.ppermute(array, ("sub", "lat"), pairs)


def swap_depths(traces):
    subs = range(lax.axis_size("sub"))
    return [traces[0]] + [
        lax.ppermute(traces[n], "sub", [(i, i ^ n) for i in subs]) for n in (1, 2, 3)
    ]


def whole(noise, colours, probe_rows, links, even, odd_inverse):
    (own,) = call(
        pack_kernel,
        "pack",
        ((50,) + noise.shape[4:],),
        (),
        (noise.reshape((48,) + noise.shape[4:]), colours),
    )
    gathered = lax.all_gather(own, "sub")
    probes_odd, turned, *sent = call(
        start_kernel,
        "start",
        (FIELD, FIELD, (12, 8, 128), (12, 8, 128)),
        (probe_rows,),
        (gathered, links[1, 3], odd_inverse),
        ((25, 2, 8, 128),),
    )
    got = (swap(sent[0], True), swap(sent[1], False))
    probes_even, partial = call(
        own_rhs_kernel,
        "own_rhs",
        (FIELD, FIELD),
        (probe_rows,),
        (gathered, turned, links),
        ((25, 2, 8, 128),),
    )
    around = call(
        around_kernel,
        "around",
        ((36, 8, 128),) * 2,
        (),
        (links, odd_inverse, turned),
        (),
        (2,),
    )
    around = (swap(around[0], True), swap(around[1], False))

    def exchange(vector, odd, far, dagger, name):
        got_far = swap(far, True)
        odd_near, near = call(
            functools.partial(near_kernel, dagger),
            "near" + name,
            (EDGE, EDGE),
            (),
            (vector, links, odd_inverse),
        )
        got_near = swap(near, False)
        direct, back = call(
            direct_kernel, "direct" + name, (FIELD, EDGE), (), (vector, even, far, near, *around)
        )
        return (direct, back, odd, odd_near, got_far, got_near, links, odd_inverse)

    vector, odd, far = call(
        rhs_kernel, "rhs", (FIELD, EDGE, EDGE), (), (partial, *got, links, odd_inverse)
    )
    kept = []
    for step in range(3):
        dagger = step % 2 == 0
        arrays = exchange(vector, odd, far, dagger, str(step))
        keep = step == 1
        vector, odd, far, *rest = call(
            functools.partial(step_kernel, dagger),
            "step%d" % step,
            (FIELD, EDGE, EDGE) + (FIELD,) * keep,
            (),
            arrays,
            () if keep else (FIELD,),
        )
        if keep:
            first_odd = rest[0]
        kept.append(vector)
    first, image, second = kept
    arrays = exchange(second, odd, far, False, "3")
    row, about = call(
        sums_kernel, "sums", ((1, 128), (8, 128)), (), (first, image, second)
    )
    early = swap_depths(
        call(
            traces_kernel,
            "traces",
            ((32, 2, 2, 128),) * 4,
            (),
            (probes_even, probes_odd, turned, first, first_odd, second),
        )
    )
    devices = lax.axis_size("lat") * lax.axis_size("sub")
    second_odd, sums = call(
        last_kernel,
        "last",
        (FIELD, (devices, 128)),
        (),
        (*arrays, image, row, about),
        (FIELD,),
    )
    sums = lax.all_to_all(sums, ("sub", "lat"), 0, 0, tiled=True)
    late = swap_depths(
        call(last_traces_kernel, "last_traces", ((8, 2, 2, 128),) * 4, (), (probes_odd, second_odd))
    )
    (out,) = call(final_kernel, "final", ((16, 2, 2, 128),), (), (sums, *early, *late))
    return out.reshape(2, 2, 4, 2, 2, 128)


def solution(mesh):
    placed = (
        P(None, None, None, None, "lat", "sub", None),
        P(None, "lat", "sub", None),
        P(),
        P(None, None, None, None, None, "lat", None, None),
        P(None, None, None, None, "lat", None, None),
        P(None, None, None, None, "lat", None, None),
    )
    return jax.shard_map(
        whole,
        mesh=mesh,
        in_specs=placed,
        out_specs=P(None, None, None, "lat", "sub", None),
        check_vma=False,
    )
```
